32 devices in a mesh: dp: 16 (over z, y, core), fsdp: 2 (over x).
Axes of the slice: x: 2, y: 2, z: 4, core: 2. Of those that a mesh axis runs over, the one named last changes fastest.
Arguments:
- tokens: bfloat16 [32, 512, 1024], P(('dp', 'fsdp')), may hold values from -6 to 6
- cotangent: bfloat16 [32, 512, 1024], P(('dp', 'fsdp')), may hold values from -6 to 6
- doc_lengths: int32 [32, 8], P(('dp', 'fsdp')), may hold values from 1 to 256, 512 in all within a row
- expand: float32 [1024, 3072], P(('dp', 'fsdp')), may hold values from -0.1875 to 0.1875
- expand_mean: float32 [1024, 3072], P(('dp', 'fsdp')), may hold values from -0.00018310547 to 0.00018310547
- expand_square: float32 [1024, 3072], P(('dp', 'fsdp')), may hold values from 3.639278e-09 to 1.4419781e-08
- contract: float32 [1536, 1024], P(('dp', 'fsdp')), may hold values from -0.625 to 0.625
- contract_mean: float32 [1536, 1024], P(('dp', 'fsdp')), may hold values from -0.00018310547 to 0.00018310547
- contract_square: float32 [1536, 1024], P(('dp', 'fsdp')), may hold values from 3.639278e-09 to 1.4419781e-08
- gating: float32 [1536, 256], P(('dp', 'fsdp')), may hold values from -0.5 to 0.5
- gating_mean: float32 [1536, 256], P(('dp', 'fsdp')), may hold values from -0.00018310547 to 0.00018310547
- gating_square: float32 [1536, 256], P(('dp', 'fsdp')), may hold values from 3.639278e-09 to 1.4419781e-08
- widen: float32 [1024, 6144], P(('dp', 'fsdp')), may hold values from -0.1875 to 0.1875
- widen_mean: float32 [1024, 6144], P(('dp', 'fsdp')), may hold values from -0.00018310547 to 0.00018310547
- widen_square: float32 [1024, 6144], P(('dp', 'fsdp')), may hold values from 3.639278e-09 to 1.4419781e-08
- narrow: float32 [3072, 1024], P(('dp', 'fsdp')), may hold values from -0.21875 to 0.21875
- narrow_mean: float32 [3072, 1024], P(('dp', 'fsdp')), may hold values from -0.00018310547 to 0.00018310547
- narrow_square: float32 [3072, 1024], P(('dp', 'fsdp')), may hold values from 3.639278e-09 to 1.4419781e-08
- scales: float32 [1024, 2], P(('dp', 'fsdp')), may hold values from 0.2 to 2
- scales_mean: float32 [1024, 2], P(('dp', 'fsdp')), may hold values from -0.0007324219 to 0.0007324219
- scales_square: float32 [1024, 2], P(('dp', 'fsdp')), may hold values from 5.836578e-08 to 2.3346313e-07
- temporal: float32 [1536, 8], P(('dp', 'fsdp')), may hold values from -2 to 4.6, as said below
- temporal_mean: float32 [1536, 8], P(('dp', 'fsdp')), may hold values from -0.0007324219 to 0.0007324219
- temporal_square: float32 [1536, 8], P(('dp', 'fsdp')), may hold values from 5.836578e-08 to 2.3346313e-07
Outputs:
- block_out: bfloat16 [32, 512, 1024], P(('dp', 'fsdp'))
- tokens_grad: bfloat16 [32, 512, 1024], P(('dp', 'fsdp'))
- grad_norm: float32 [], replicated
- expand_after: float32 [1024, 3072], P(('dp', 'fsdp'))
- expand_means: float32 [1024, 3072], P(('dp', 'fsdp'))
- expand_squares: float32 [1024, 3072], P(('dp', 'fsdp'))
- contract_after: float32 [1536, 1024], P(('dp', 'fsdp'))
- contract_means: float32 [1536, 1024], P(('dp', 'fsdp'))
- contract_squares: float32 [1536, 1024], P(('dp', 'fsdp'))
- gating_after: float32 [1536, 256], P(('dp', 'fsdp'))
- gating_means: float32 [1536, 256], P(('dp', 'fsdp'))
- gating_squares: float32 [1536, 256], P(('dp', 'fsdp'))
- widen_after: float32 [1024, 6144], P(('dp', 'fsdp'))
- widen_means: float32 [1024, 6144], P(('dp', 'fsdp'))
- widen_squares: float32 [1024, 6144], P(('dp', 'fsdp'))
- narrow_after: float32 [3072, 1024], P(('dp', 'fsdp'))
- narrow_means: float32 [3072, 1024], P(('dp', 'fsdp'))
- narrow_squares: float32 [3072, 1024], P(('dp', 'fsdp'))
- scales_after: float32 [1024, 2], P(('dp', 'fsdp'))
- scales_means: float32 [1024, 2], P(('dp', 'fsdp'))
- scales_squares: float32 [1024, 2], P(('dp', 'fsdp'))
- temporal_after: float32 [1536, 8], P(('dp', 'fsdp'))
- temporal_means: float32 [1536, 8], P(('dp', 'fsdp'))
- temporal_squares: float32 [1536, 8], P(('dp', 'fsdp'))
The draws below stay inside these ranges and needn't reach their ends.
Inputs may be any that keep to these rules, and one draw needn't show every extreme that they name: `doc_lengths`: each row's 8 lengths sum to 512, and each row holds a document of exactly 256 tokens. `temporal`: column 7 lies within 2.2 to 4.6.
All inputs are finite; a program needn't handle non-finite values.
Results may differ from the reference program's by a relative error of at most 0.012.
The reference program's roundings to bfloat16 on the way count: a program that leaves them out, or rounds other values in their place, can miss the bound.
Values may be sent and summed in bfloat16 or wider, within the bound.
A program may use at most 320 MiB of HBM per device.

```python
import math
import jax
import jax.numpy as jnp
import numpy as np
from jax import lax

D = 1024
R = 1536
FF = 3072
HW = 128
LEN = 512
NDOC = 8
STEP = 10
ROWS = 32
NPARAM = 14563328


def draw_scales(key, part):
    key = jax.random.fold_in(key, 11)
    place = jnp.arange(D, dtype=jnp.float32)[:, None] / (D - 1)
    ramp = 0.5 + place
    noise = jax.random.uniform(key, (D, 2), jnp.float32, 0.8, 1.2)
    return ramp * noise


def draw_temporal(key, part):
    key = jax.random.fold_in(key, 23)
    first_key, second_key = jax.random.split(key)
    mixed = jnp.clip(0.5 * jax.random.normal(first_key, (R, 7), jnp.float32), -2.0, 2.0)
    decay_param = jax.random.uniform(second_key, (R, 1), jnp.float32, 2.2, 4.6)
    return jnp.concatenate([mixed, decay_param], axis=1)


def level_of(key, shape, cuts, smallest, top_value):
    factor_of = 1.0
    for axis_at, shards_of in cuts:
        draws = jax.random.uniform(jax.random.fold_in(jax.random.fold_in(key, 6), axis_at), (shards_of,), jnp.float32, smallest / len(cuts), top_value / len(cuts))
        factor_of = factor_of * jnp.repeat(jnp.exp(draws), shape[axis_at] // shards_of).reshape((-1,) + (1,) * (len(shape) - 1 - axis_at))
    return factor_of


def split_up(count, total, bound, slope):
    loads = [(1 << 20) // math.isqrt(rank ** slope) + 1 for rank in range(2, count + 1)]
    spare, holding = total - bound - (count - 1), [1] * (count - 1)
    while spare > 0:
        free = [i for i in range(count - 1) if holding[i] < bound]
        pool, left = sum([loads[i] for i in free]), spare
        for i in free:
            addition = min(bound - holding[i], max(1, left * loads[i] // pool), spare)
            holding[i] = holding[i] + addition
            spare = spare - addition
    return np.array([bound] + holding)


def uneven(rng, count, total, limit, skew):
    if count == 2:
        one = jax.random.randint(rng, (), max(1, total - limit), min(limit, total - 1) + 1)
        return jnp.stack([one, total - one])
    sizes = jnp.asarray(split_up(count, total, limit, skew), jnp.int32)
    couples = (count - 1) // 2
    donor, taker = sizes[1:1 + 2 * couples:2], sizes[2:2 + 2 * couples:2]
    slack = jnp.minimum(donor - 1, limit - taker)
    moved = jax.random.randint(jax.random.fold_in(rng, 1), (couples,), 0, 1 << 20) % (slack + 1)
    sizes = sizes.at[1:1 + 2 * couples:2].set(donor - moved).at[2:2 + 2 * couples:2].set(taker + moved)
    return sizes[jax.random.permutation(jax.random.fold_in(rng, 2), count)]


def scatter_about(own_key, dims, scale, reach, pieces=(), held_as=jnp.bfloat16):
    result = scale * jax.random.normal(own_key, dims, jnp.float32)
    if pieces:
        result = result * level_of(own_key, dims, pieces, -0.22, 0.18)
    return jnp.clip(result, -reach, reach).astype(held_as)


def setup_inputs(seed: int = 0) -> dict:
    streams_of = jax.random.split(jax.random.key(seed), 25)
    tokens = scatter_about(streams_of[0], (ROWS, LEN, D), 1.0, 6.0, ((0, 32),))
    cotangent = scatter_about(streams_of[1], (ROWS, LEN, D), 1.0, 6.0, ((0, 32),))
    doc_lengths = jax.vmap(lambda own: uneven(own, NDOC, LEN, LEN // 2, 2))(jax.random.split(streams_of[2], ROWS)).reshape((ROWS, NDOC)).astype(jnp.int32)
    expand = scatter_about(streams_of[3], (D, 2 * R), D ** -0.5, 0.1875, ((0, 32),), jnp.float32)
    expand_mean = scatter_about(streams_of[4], (D, 2 * R), (0.11 * NPARAM ** -0.5), 0.00018310547, ((0, 32),), jnp.float32)
    expand_square = jnp.clip(jnp.exp(math.log(1.4419780924868064e-08) - 1.37681563 * jax.random.uniform(streams_of[5], (D, 2 * R), jnp.float32) ** level_of(streams_of[5], (D, 2 * R), ((0, 32),), -0.2, 0.2)), 3.6392779900751293e-09, 1.4419780924868064e-08)
    contract = scatter_about(streams_of[6], (R, D), (R // 16) ** -0.5, 0.625, ((0, 32),), jnp.float32)
    contract_mean = scatter_about(streams_of[7], (R, D), (0.11 * NPARAM ** -0.5), 0.00018310547, ((0, 32),), jnp.float32)
    contract_square = jnp.clip(jnp.exp(math.log(1.4419780924868064e-08) - 1.37681563 * jax.random.uniform(streams_of[8], (R, D), jnp.float32) ** level_of(streams_of[8], (R, D), ((0, 32),), -0.2, 0.2)), 3.6392779900751293e-09, 1.4419780924868064e-08)
    gating = scatter_about(streams_of[9], (R, 2 * HW), HW ** -0.5, 0.5, ((0, 32),), jnp.float32)
    gating_mean = scatter_about(streams_of[10], (R, 2 * HW), (0.11 * NPARAM ** -0.5), 0.00018310547, ((0, 32),), jnp.float32)
    gating_square = jnp.clip(jnp.exp(math.log(1.4419780924868064e-08) - 1.37681563 * jax.random.uniform(streams_of[11], (R, 2 * HW), jnp.float32) ** level_of(streams_of[11], (R, 2 * HW), ((0, 32),), -0.2, 0.2)), 3.6392779900751293e-09, 1.4419780924868064e-08)
    widen = scatter_about(streams_of[12], (D, 2 * FF), D ** -0.5, 0.1875, ((0, 32),), jnp.float32)
    widen_mean = scatter_about(streams_of[13], (D, 2 * FF), (0.11 * NPARAM ** -0.5), 0.00018310547, ((0, 32),), jnp.float32)
    widen_square = jnp.clip(jnp.exp(math.log(1.4419780924868064e-08) - 1.37681563 * jax.random.uniform(streams_of[14], (D, 2 * FF), jnp.float32) ** level_of(streams_of[14], (D, 2 * FF), ((0, 32),), -0.2, 0.2)), 3.6392779900751293e-09, 1.4419780924868064e-08)
    narrow = scatter_about(streams_of[15], (FF, D), (FF // 4) ** -0.5, 0.21875, ((0, 32),), jnp.float32)
    narrow_mean = scatter_about(streams_of[16], (FF, D), (0.11 * NPARAM ** -0.5), 0.00018310547, ((0, 32),), jnp.float32)
    narrow_square = jnp.clip(jnp.exp(math.log(1.4419780924868064e-08) - 1.37681563 * jax.random.uniform(streams_of[17], (FF, D), jnp.float32) ** level_of(streams_of[17], (FF, D), ((0, 32),), -0.2, 0.2)), 3.6392779900751293e-09, 1.4419780924868064e-08)
    scales = draw_scales(jax.random.fold_in(streams_of[24], 71), 0)
    scales_mean = scatter_about(streams_of[19], (D, 2), (0.44 * NPARAM ** -0.5), 0.0007324219, ((0, 32),), jnp.float32)
    scales_square = jnp.clip(jnp.exp(math.log(2.3346312616467912e-07) - 1.3862944 * jax.random.uniform(streams_of[20], (D, 2), jnp.float32) ** level_of(streams_of[20], (D, 2), ((0, 32),), -0.2, 0.2)), 5.836578154116978e-08, 2.3346312616467912e-07)
    temporal = draw_temporal(jax.random.fold_in(streams_of[24], 71), 0)
    temporal_mean = scatter_about(streams_of[22], (R, 8), (0.44 * NPARAM ** -0.5), 0.0007324219, ((0, 32),), jnp.float32)
    temporal_square = jnp.clip(jnp.exp(math.log(2.3346312616467912e-07) - 1.3862944 * jax.random.uniform(streams_of[23], (R, 8), jnp.float32) ** level_of(streams_of[23], (R, 8), ((0, 32),), -0.2, 0.2)), 5.836578154116978e-08, 2.3346312616467912e-07)
    return dict(tokens=tokens, cotangent=cotangent, doc_lengths=doc_lengths, expand=expand, expand_mean=expand_mean, expand_square=expand_square, contract=contract, contract_mean=contract_mean, contract_square=contract_square, gating=gating, gating_mean=gating_mean, gating_square=gating_square, widen=widen, widen_mean=widen_mean, widen_square=widen_square, narrow=narrow, narrow_mean=narrow_mean, narrow_square=narrow_square, scales=scales, scales_mean=scales_mean, scales_square=scales_square, temporal=temporal, temporal_mean=temporal_mean, temporal_square=temporal_square)


NORM_EPSILON = 1e-06
GATE_POWER = 8.0
BETA_FIRST = 0.9
BETA_SECOND = 0.95
ADAM_EPSILON = 1e-08
RATE_MATRIX = 0.1
RATE_VECTOR = 1.0
WEIGHT_DECAY = 0.1
CLIP_NORM = 1.0
HIGH = lax.Precision.HIGHEST

@jax.custom_vjp
def low(v):
    return lax.optimization_barrier(v.astype(jnp.bfloat16)).astype(jnp.float32)

@jax.custom_vjp
def low_back(v):
    return v

def low_keep(v):
    return (low(v), None)

def low_pass(kept, grad):
    return (grad,)

def back_keep(v):
    return (v, None)

def back_low(kept, grad):
    return (low(grad),)
low.defvjp(low_keep, low_pass)
low_back.defvjp(back_keep, back_low)

def rms_scale(values, weights):
    return values * lax.rsqrt(lax.optimization_barrier(jnp.mean(values * values, axis=-1, keepdims=True)) + NORM_EPSILON) * weights

def doc_tables(lengths, length):
    starts = (jnp.cumsum(lengths, axis=-1) - lengths).astype(jnp.int32)
    places = jnp.arange(length, dtype=jnp.int32)
    matches = places[:, None] == starts[..., None, :]
    resets = jnp.any(matches, axis=-1).astype(jnp.float32)
    segment = lax.optimization_barrier(jnp.sum((starts[..., None, :] <= places[:, None]).astype(jnp.int32), axis=-1)).astype(jnp.int32)
    return (resets, segment)

def causal_conv(inputs, conv_taps, conv_bias, segment):
    length = inputs.shape[-2]
    running = conv_bias + inputs * conv_taps[:, 0]
    for offset in range(1, 4):
        shifted = jnp.concatenate([jnp.zeros_like(inputs[..., :offset, :]), inputs[..., :length - offset, :]], axis=-2)
        earlier_segment = jnp.concatenate([jnp.full_like(segment[..., :offset], -1), segment[..., :length - offset]], axis=-1)
        keeping = (earlier_segment == segment).astype(jnp.float32)[..., None]
        running = running + shifted * conv_taps[:, offset] * keeping
    return running

def combine_linear(earlier, later):
    return (earlier[0] * later[0], later[0] * earlier[1] + later[1])

def recurrence(decays, inputs):
    return lax.associative_scan(combine_linear, (decays, inputs), axis=-2)[1]

def temporal_mix(gate_logits, branch_logits, conv_values, recur_bias, resets):
    head_width = gate_logits.shape[-1] // 2
    flat_shape = branch_logits.shape
    recur_logit = gate_logits[..., :head_width].reshape(flat_shape) + recur_bias[:, 0]
    input_logit = gate_logits[..., head_width:].reshape(flat_shape) + recur_bias[:, 1]
    recur_gate = jax.nn.sigmoid(recur_logit)
    input_gate = jax.nn.sigmoid(input_logit)
    log_decay = -GATE_POWER * recur_gate * jax.nn.softplus(-recur_bias[:, 2])
    carried = 1.0 - resets[..., None]
    decays = jnp.exp(log_decay) * carried
    scaling = jnp.sqrt(-jnp.expm1(2.0 * log_decay)) * carried + resets[..., None]
    states = recurrence(decays, scaling * input_gate * conv_values)
    return states * jax.nn.gelu(branch_logits)

def block_forward(inputs, expand, contract, gating, widen, narrow, scales, temporal, resets, segment):
    expand = low(expand)
    contract = low(contract)
    gating = low(gating)
    widen = low(widen)
    narrow = low(narrow)
    scales = low(scales)
    temporal = low(temporal)
    width = contract.shape[0]
    hidden = narrow.shape[0]
    head_width = gating.shape[1] // 2
    head_count = width // head_width
    normed = low(rms_scale(inputs, scales[:, 0]))
    projected = low_back(jnp.einsum('bld,dr->blr', normed, expand, precision=HIGH))
    conv_low = low(causal_conv(projected[..., :width], temporal[:, 0:4], temporal[:, 4], segment))
    blocks = conv_low.reshape(conv_low.shape[:-1] + (head_count, head_width))
    gating_blocks = gating.reshape(head_count, head_width, 2 * head_width)
    gate_logits = low_back(jnp.einsum('blhk,hkj->blhj', blocks, gating_blocks, precision=HIGH))
    mixed = low(temporal_mix(gate_logits, projected[..., width:], conv_low, temporal[:, 5:8], resets))
    middle = inputs + low_back(jnp.einsum('blr,rd->bld', mixed, contract, precision=HIGH))
    normed_two = low(rms_scale(middle, scales[:, 1]))
    widened = low_back(jnp.einsum('bld,df->blf', normed_two, widen, precision=HIGH))
    activated = low(jax.nn.gelu(widened[..., :hidden]) * widened[..., hidden:])
    return middle + jnp.einsum('blf,fd->bld', activated, narrow, precision=HIGH)

def adam_update(master, moment_one, moment_two, gradient, factor, rate, decay):
    clipped = gradient * factor
    new_one = BETA_FIRST * moment_one + (1.0 - BETA_FIRST) * clipped
    new_two = BETA_SECOND * moment_two + (1.0 - BETA_SECOND) * clipped * clipped
    first_hat = new_one / (1.0 - BETA_FIRST ** STEP)
    second_hat = new_two / (1.0 - BETA_SECOND ** STEP)
    after = master - rate * (first_hat / (jnp.sqrt(second_hat) + ADAM_EPSILON) + decay * master)
    return (after, new_one, new_two)

def reference(tokens, cotangent, doc_lengths, expand, expand_mean, expand_square, contract, contract_mean, contract_square, gating, gating_mean, gating_square, widen, widen_mean, widen_square, narrow, narrow_mean, narrow_square, scales, scales_mean, scales_square, temporal, temporal_mean, temporal_square):
    weights_all = (expand, contract, gating, widen, narrow, scales, temporal)
    row_count = tokens.shape[0]
    length = tokens.shape[1]
    group_rows = min(row_count, max(1, 4096 // length))
    group_count = row_count // group_rows

    def grouped(array):
        return array.reshape((group_count, group_rows) + array.shape[1:])

    def one_group(totals, blocked):
        block_tokens, block_cotangent, block_lengths = blocked
        resets, segment = doc_tables(block_lengths, length)

        def forward(inputs, *weights):
            return block_forward(inputs, *weights, resets, segment)
        outputs, pullback = jax.vjp(forward, block_tokens.astype(jnp.float32), *weights_all)
        grads = pullback(block_cotangent.astype(jnp.float32))
        totals = tuple((running + update for running, update in zip(totals, grads[1:])))
        return (totals, (outputs.astype(jnp.bfloat16), grads[0].astype(jnp.bfloat16)))
    zeros = tuple((jnp.zeros_like(weight) for weight in weights_all))
    totals, results = lax.scan(one_group, zeros, (grouped(tokens), grouped(cotangent), grouped(doc_lengths)))
    block_out = results[0].reshape(tokens.shape)
    tokens_grad = results[1].reshape(tokens.shape)
    squares = jnp.float32(0.0)
    for gradient in totals:
        squares = squares + jnp.sum(gradient * gradient)
    grad_norm = jnp.sqrt(squares)
    factor = CLIP_NORM / jnp.maximum(grad_norm, CLIP_NORM)
    moments = ((expand_mean, expand_square), (contract_mean, contract_square), (gating_mean, gating_square), (widen_mean, widen_square), (narrow_mean, narrow_square), (scales_mean, scales_square), (temporal_mean, temporal_square))
    updated = []
    for index in range(7):
        rate = RATE_MATRIX if index < 5 else RATE_VECTOR
        decay = WEIGHT_DECAY if index < 5 else 0.0
        updated.append(adam_update(weights_all[index], moments[index][0], moments[index][1], totals[index], factor, rate, decay))
    return (block_out, tokens_grad, grad_norm, updated[0][0], updated[0][1], updated[0][2], updated[1][0], updated[1][1], updated[1][2], updated[2][0], updated[2][1], updated[2][2], updated[3][0], updated[3][1], updated[3][2], updated[4][0], updated[4][1], updated[4][2], updated[5][0], updated[5][1], updated[5][2], updated[6][0], updated[6][1], updated[6][2])
```

```python
import functools

import jax
import jax.numpy as jnp
from jax import lax
from jax.experimental import pallas as pl
from jax.experimental.pallas import tpu as pltpu
from jax.sharding import PartitionSpec as P

STEP = 10


NORM_EPSILON = 1e-06
GATE_POWER = 8.0
BETA_FIRST = 0.9
BETA_SECOND = 0.95
ADAM_EPSILON = 1e-08
RATE_MATRIX = 0.1
RATE_VECTOR = 1.0
WEIGHT_DECAY = 0.1
CLIP_NORM = 1.0


MESH = pl.DeviceIdType.MESH
BRAIN = jnp.bfloat16
VMEM_BYTES = 60 * 1024 * 1024


def bit_count(size):
    return size.bit_length() - 1


class Cube:
    def __init__(self, mesh_shape):
        self.dp = bit_count(mesh_shape["dp"])
        self.fsdp = bit_count(mesh_shape["fsdp"])
        self.bits = self.dp + self.fsdp
        self.core = self.dp - 1

    def place(self):
        outer, inner = lax.axis_index("dp"), lax.axis_index("fsdp")
        bits = [lax.rem(outer // (1 << (self.dp - 1 - i)), 2) for i in range(self.dp)]
        return bits + [lax.rem(inner // (1 << (self.fsdp - 1 - i)), 2) for i in range(self.fsdp)]

    def partner(self, place, bit):
        outer, inner = lax.axis_index("dp"), lax.axis_index("fsdp")
        flip = 1 - 2 * place[bit]
        if bit < self.dp:
            return (outer + flip * (1 << (self.dp - 1 - bit)), inner)
        return (outer, inner + flip * (1 << (self.bits - 1 - bit)))

    def orders(self):
        rest = [i for i in range(self.bits) if i != self.core]
        last = rest[-1]
        across = rest[-2]
        lines = rest[:-2]
        return [
            [last] + lines + [across, self.core],
            [across] + lines + [last, self.core],
            lines + [across, last, self.core],
            lines + [last, across, self.core],
        ]


def greet(cube, place):
    barrier = pltpu.get_barrier_semaphore()
    for bit in range(cube.bits):
        pl.semaphore_signal(barrier, inc=1, device_id=cube.partner(place, bit), device_id_type=MESH)
    pl.semaphore_wait(barrier, cube.bits)


def cut_pieces(cube, widths, groups):
    orders = cube.orders()
    pieces = []
    for array, width in enumerate(widths):
        first = 0
        for group, share in groups[array]:
            for columns, order in zip(share, orders):
                if columns:
                    pieces.append((group, array, first, columns * 128, order))
                    first += columns * 128
        assert first == width
    return sorted(pieces, key=lambda piece: piece[0])


def gather_kernel(cube, pieces, count, *refs):
    sources, fulls = refs[:count], refs[count : 2 * count]
    held, own_sem, send_sem, recv_sem = (
        refs[2 * count : 3 * count],
        refs[3 * count],
        refs[3 * count + 1],
        refs[3 * count + 2],
    )
    place = cube.place()
    greet(cube, place)
    own = []
    for i in range(count):
        held[i][...] = sources[i][...].astype(held[i].dtype)
        copy = pltpu.make_async_copy(held[i], fulls[i].at[tuple(place)], own_sem.at[i])
        copy.start()
        own.append(copy)
    for copy in own:
        copy.wait()

    def exchange(number, stage):
        _, array, first, columns, order = pieces[number]
        spot = tuple(
            slice(None) if bit in order[:stage] else place[bit] for bit in range(cube.bits)
        )
        view = fulls[array].at[spot + (slice(None), pl.ds(first, columns))]
        return pltpu.make_async_remote_copy(
            src_ref=view,
            dst_ref=view,
            send_sem=send_sem.at[number, stage],
            recv_sem=recv_sem.at[number, stage],
            device_id=cube.partner(place, order[stage]),
            device_id_type=MESH,
        )

    for slot in range(pieces[-1][0] + cube.bits + 1):
        for number in range(len(pieces)):
            stage = slot - pieces[number][0]
            if 0 <= stage <= cube.bits:
                if stage > 0:
                    exchange(number, stage - 1).wait_recv()
                if stage < cube.bits:
                    exchange(number, stage).start()
    for number in range(len(pieces)):
        for stage in range(cube.bits):
            exchange(number, stage).wait_send()


def gather_all(cube, shards_in, kinds, groups):
    count = len(shards_in)
    pieces = cut_pieces(cube, [s.shape[1] for s in shards_in], groups)
    fulls = [(2,) * cube.bits + s.shape for s in shards_in]
    gathered = pl.pallas_call(
        functools.partial(gather_kernel, cube, pieces, count),
        out_shape=[jax.ShapeDtypeStruct(shape, kind) for shape, kind in zip(fulls, kinds)],
        in_specs=[pl.BlockSpec(memory_space=pltpu.VMEM)] * count,
        out_specs=[pl.BlockSpec(memory_space=pl.ANY)] * count,
        scratch_shapes=[pltpu.VMEM(s.shape, kind) for s, kind in zip(shards_in, kinds)]
        + [
            pltpu.SemaphoreType.DMA((count,)),
            pltpu.SemaphoreType.DMA((len(pieces), cube.bits)),
            pltpu.SemaphoreType.DMA((len(pieces), cube.bits)),
        ],
        compiler_params=pltpu.CompilerParams(
            collective_id=0, has_side_effects=True, vmem_limit_bytes=VMEM_BYTES
        ),
    )(*shards_in)
    return [g.reshape((-1,) + g.shape[cube.bits + 1 :]) for g in gathered]


def scatter_kernel(cube, pieces, count, *refs):
    grads, sums = refs[:count], refs[count : 2 * count]
    norm = refs[2 * count]
    refs = refs[2 * count + 1 :]
    held = refs[:count]
    inbox = [
        refs[(1 + stage) * count : (2 + stage) * count] for stage in range(cube.bits)
    ]
    own_sem, send_sem, recv_sem, partial, other, norm_send, norm_recv = refs[
        (1 + cube.bits) * count :
    ]
    place = cube.place()
    greet(cube, place)

    def bits_left(number, stage):
        order = pieces[number][4]
        return [bit for bit in range(cube.bits) if bit not in order[cube.bits - stage :]]

    def own_copy(number):
        _, array, first, columns, order = pieces[number]
        spot = tuple(place[bit] if bit == order[-1] else slice(None) for bit in range(cube.bits))
        window = (slice(None), pl.ds(first, columns))
        rest = (slice(None),) * (cube.bits - 1)
        return pltpu.make_async_copy(
            grads[array].at[spot + window], held[array].at[rest + window], own_sem.at[number]
        )

    def exchange(number, stage):
        _, array, first, columns, order = pieces[number]
        bit = order[cube.bits - 1 - stage]
        left = bits_left(number, stage)
        source = grads[array] if stage == 0 else inbox[stage - 1][array]
        spot = tuple(1 - place[bit] if b == bit else slice(None) for b in left)
        window = (slice(None), pl.ds(first, columns))
        rest = (slice(None),) * (len(left) - 1)
        return pltpu.make_async_remote_copy(
            src_ref=source.at[spot + window],
            dst_ref=inbox[stage][array].at[rest + window],
            send_sem=send_sem.at[number, stage],
            recv_sem=recv_sem.at[number, stage],
            device_id=cube.partner(place, bit),
            device_id_type=MESH,
        )

    def add(number, stage):
        _, array, first, columns, order = pieces[number]
        bit = order[cube.bits - 1 - stage]
        left = bits_left(number, stage)
        after = [b for b in left if b != bit]
        window = (slice(None), pl.ds(first, columns))
        target = inbox[stage][array]

        def one(step, carry):
            spot = tuple(
                lax.rem(step // (1 << (len(after) - 1 - i)), 2) for i in range(len(after))
            )
            if stage == 0:
                mine = held[array][spot + window]
            else:
                mixed = list(spot)
                mixed.insert(left.index(bit), place[bit])
                mine = inbox[stage - 1][array][tuple(mixed) + window]
            total = mine.astype(jnp.float32) + target[spot + window].astype(jnp.float32)
            if stage == cube.bits - 1:
                sums[array][window] = total
                squares = total * total
                tile = squares.reshape(squares.shape[0] // 8, 8, columns).sum(axis=0)
                for start in range(0, columns, 128):
                    partial[0] += tile[:, start : start + 128]
            else:
                target[spot + window] = total.astype(target.dtype)
            return carry

        lax.fori_loop(0, 1 << len(after), one, 0)

    partial[0] = jnp.zeros(partial.shape[1:], jnp.float32)
    for number in range(len(pieces)):
        own_copy(number).start()
    for slot in range(pieces[-1][0] + cube.bits + 1):
        for number in range(len(pieces)):
            stage = slot - pieces[number][0]
            if 0 <= stage <= cube.bits:
                if stage > 0:
                    if stage == 1:
                        own_copy(number).wait()
                    exchange(number, stage - 1).wait_recv()
                    add(number, stage - 1)
                if stage < cube.bits:
                    exchange(number, stage).start()
    for number in range(len(pieces)):
        for stage in range(cube.bits):
            exchange(number, stage).wait_send()
    for bit in range(cube.bits):
        copy = pltpu.make_async_remote_copy(
            src_ref=partial.at[bit],
            dst_ref=other.at[bit],
            send_sem=norm_send.at[bit],
            recv_sem=norm_recv.at[bit],
            device_id=cube.partner(place, bit),
            device_id_type=MESH,
        )
        copy.start()
        copy.wait()
        if bit < cube.bits - 1:
            partial[bit + 1] = partial[bit] + other[bit]
        else:
            norm[...] = partial[bit] + other[bit]


def scatter_all(cube, grads, groups):
    count = len(grads)
    devices = 1 << cube.bits
    shapes = [(g.shape[0] // devices, g.shape[1]) for g in grads]
    pieces = cut_pieces(cube, [g.shape[1] for g in grads], groups)
    scratch = [
        pltpu.VMEM((2,) * (cube.bits - 1) + shape, g.dtype) for shape, g in zip(shapes, grads)
    ]
    for stage in range(cube.bits):
        scratch += [
            pltpu.VMEM((2,) * (cube.bits - 1 - stage) + shape, g.dtype)
            for shape, g in zip(shapes, grads)
        ]
    return pl.pallas_call(
        functools.partial(scatter_kernel, cube, pieces, count),
        out_shape=[jax.ShapeDtypeStruct(shape, jnp.float32) for shape in shapes + [(8, 128)]],
        in_specs=[pl.BlockSpec(memory_space=pl.ANY)] * count,
        out_specs=[pl.BlockSpec(memory_space=pltpu.VMEM)] * (count + 1),
        scratch_shapes=scratch
        + [
            pltpu.SemaphoreType.DMA((len(pieces),)),
            pltpu.SemaphoreType.DMA((len(pieces), cube.bits)),
            pltpu.SemaphoreType.DMA((len(pieces), cube.bits)),
            pltpu.VMEM((cube.bits, 8, 128), jnp.float32),
            pltpu.VMEM((cube.bits, 8, 128), jnp.float32),
            pltpu.SemaphoreType.DMA((cube.bits,)),
            pltpu.SemaphoreType.DMA((cube.bits,)),
        ],
        compiler_params=pltpu.CompilerParams(
            collective_id=1, has_side_effects=True, vmem_limit_bytes=VMEM_BYTES
        ),
    )(*[g.reshape((2,) * cube.bits + s) for g, s in zip(grads, shapes)])


GROUPS = (
    ((0, (0, 0, 1, 0)),),
    ((0, (2, 2, 4, 4)), (1, (2, 2, 4, 4))),
    ((2, (0, 0, 1, 1)),),
    ((2, (1, 1, 3, 3)),),
    ((3, (2, 2, 4, 4)), (4, (2, 2, 4, 4)), (5, (2, 2, 4, 4)), (6, (2, 2, 4, 4))),
    ((7, (1, 1, 1, 1)), (8, (1, 1, 1, 1))),
)
AXES = ("dp", "fsdp")


def pack_vectors(temporal, scales):
    upper = jnp.concatenate([temporal.T, jnp.pad(scales.T, ((0, 6), (0, 0)))], axis=1)
    return jnp.pad(upper, ((0, 0), (0, 128 - upper.shape[1])))


def gather_params(cube, misc, matrices):
    if all(m.shape[0] % 16 == 0 for m in matrices):
        kinds = [jnp.float32] + [BRAIN] * len(matrices)
        return gather_all(cube, [misc] + list(matrices), kinds, GROUPS)
    sent = [misc] + [m.astype(BRAIN) for m in matrices]
    return [lax.all_gather(v, AXES, axis=0, tiled=True) for v in sent]


def scatter_grads(cube, misc, grads):
    if all((g.shape[0] >> cube.bits) % 16 == 0 for g in grads):
        outs = scatter_all(cube, [misc] + list(grads), GROUPS)
        return outs[:-1], outs[-1]
    sums = [
        lax.psum_scatter(g.astype(jnp.float32), AXES, scatter_dimension=0, tiled=True)
        for g in [misc] + list(grads)
    ]
    squares = lax.psum(sum(jnp.sum(s * s) for s in sums), AXES)
    return sums, jnp.pad(squares[None, None], ((0, 7), (0, 127)))


def adam_kernel(count, norm_tile, *refs):
    grads, olds, ones, twos = (refs[i * count : (i + 1) * count] for i in range(4))
    norm_ref = refs[4 * count]
    afters, new_ones, new_twos = (
        refs[4 * count + 1 + i * count : 4 * count + 1 + (i + 1) * count] for i in range(3)
    )
    grad_norm = jnp.sqrt(jnp.sum(norm_tile[...], keepdims=True))
    norm_ref[...] = grad_norm
    factor = CLIP_NORM / jnp.maximum(grad_norm, CLIP_NORM)
    for i in range(count):
        matrix = i < count - 2
        after, one, two = adam_update(
            olds[i][...],
            ones[i][...],
            twos[i][...],
            grads[i][...],
            factor,
            RATE_MATRIX if matrix else RATE_VECTOR,
            WEIGHT_DECAY if matrix else 0.0,
        )
        afters[i][...] = after
        new_ones[i][...] = one
        new_twos[i][...] = two


def adam_all(norm_tile, grads, olds, ones, twos):
    count = len(grads)
    like = [jax.ShapeDtypeStruct(v.shape, v.dtype) for v in olds]
    return pl.pallas_call(
        functools.partial(adam_kernel, count),
        out_shape=[jax.ShapeDtypeStruct((1, 1), jnp.float32)] + like * 3,
        compiler_params=pltpu.CompilerParams(vmem_limit_bytes=VMEM_BYTES),
    )(norm_tile, *grads, *olds, *ones, *twos)


def rms_scale(values, weights):
    return (
        values
        * lax.rsqrt(jnp.mean(values * values, axis=-1, keepdims=True) + NORM_EPSILON)
        * weights
    )


def doc_tables(lengths, length):
    starts = jnp.cumsum(lengths, axis=-1) - lengths
    places = jnp.arange(length, dtype=jnp.int32)
    matches = places[:, None] == starts[..., None, :]
    resets = jnp.any(matches, axis=-1).astype(jnp.float32)
    segment = jnp.sum((starts[..., None, :] <= places[:, None]).astype(jnp.int32), axis=-1)
    return (resets, segment)


def causal_conv(inputs, conv_taps, conv_bias, segment):
    length = inputs.shape[-2]
    running = conv_bias + inputs * conv_taps[:, 0]
    for offset in range(1, 4):
        shifted = jnp.concatenate(
            [jnp.zeros_like(inputs[..., :offset, :]), inputs[..., : length - offset, :]], axis=-2
        )
        earlier_segment = jnp.concatenate(
            [jnp.full_like(segment[..., :offset], -1), segment[..., : length - offset]], axis=-1
        )
        keeping = (earlier_segment == segment).astype(jnp.float32)[..., None]
        running = running + shifted * conv_taps[:, offset] * keeping
    return running


def combine_linear(earlier, later):
    return (earlier[0] * later[0], later[0] * earlier[1] + later[1])


def recurrence(decays, inputs):
    return lax.associative_scan(combine_linear, (decays, inputs), axis=-2)[1]


def temporal_mix(gate_logits, branch_logits, conv_values, recur_bias, resets):
    head_width = gate_logits.shape[-1] // 2
    flat_shape = branch_logits.shape
    recur_logit = gate_logits[..., :head_width].reshape(flat_shape) + recur_bias[:, 0]
    input_logit = gate_logits[..., head_width:].reshape(flat_shape) + recur_bias[:, 1]
    recur_gate = jax.nn.sigmoid(recur_logit)
    input_gate = jax.nn.sigmoid(input_logit)
    log_decay = -GATE_POWER * recur_gate * jax.nn.softplus(-recur_bias[:, 2])
    carried = 1.0 - resets[..., None]
    decays = jnp.exp(log_decay) * carried
    scaling = jnp.sqrt(-jnp.expm1(2.0 * log_decay)) * carried + resets[..., None]
    states = recurrence(decays, scaling * input_gate * conv_values)
    return states * jax.nn.gelu(branch_logits)


def product_rows(former, latter):
    return lax.dot_general(
        former, latter, (((0,), (0,)), ((), ())), preferred_element_type=jnp.float32
    )


def product_cols(former, latter):
    return lax.dot_general(
        former, latter, (((1,), (1,)), ((), ())), preferred_element_type=jnp.float32
    )


def adam_update(master, moment_one, moment_two, gradient, factor, rate, decay):
    clipped = gradient * factor
    new_one = BETA_FIRST * moment_one + (1.0 - BETA_FIRST) * clipped
    new_two = BETA_SECOND * moment_two + (1.0 - BETA_SECOND) * clipped * clipped
    first_hat = new_one / (1.0 - BETA_FIRST**STEP)
    second_hat = new_two / (1.0 - BETA_SECOND**STEP)
    after = master - rate * (first_hat / (jnp.sqrt(second_hat) + ADAM_EPSILON) + decay * master)
    return (after, new_one, new_two)


def shards(
    cube,
    tokens,
    cotangent,
    doc_lengths,
    expand,
    expand_mean,
    expand_square,
    contract,
    contract_mean,
    contract_square,
    gating,
    gating_mean,
    gating_square,
    widen,
    widen_mean,
    widen_square,
    narrow,
    narrow_mean,
    narrow_square,
    scales,
    scales_mean,
    scales_square,
    temporal,
    temporal_mean,
    temporal_square,
):
    brain = jnp.bfloat16
    rows_t, rows_s = temporal.shape[0], scales.shape[0]
    vectors = pack_vectors(temporal, scales).astype(brain).astype(jnp.float32)
    vectors, expand_full, gating_full, contract_full, widen_full, narrow_full = gather_params(
        cube, vectors, (expand, gating, contract, widen, narrow)
    )
    vectors = vectors.reshape(-1, 8, 128).transpose(0, 2, 1)
    temporal_float = vectors[:, :rows_t].reshape(-1, 8)
    scales_float = vectors[:, rows_t : rows_t + rows_s, :2].reshape(-1, 2)
    width = contract_full.shape[0]
    hidden = narrow_full.shape[0]
    head_width = gating_full.shape[1] // 2
    head_count = width // head_width
    length = tokens.shape[1]
    resets, segment = doc_tables(doc_lengths, length)
    resets = resets[0]
    segment = segment[0]
    inputs = tokens[0].astype(jnp.float32)
    normed, norm_pull = jax.vjp(rms_scale, inputs, scales_float[:, 0])
    normed_low = normed.astype(brain)
    projected = jnp.dot(normed_low, expand_full, preferred_element_type=jnp.float32)

    def conv_piece(values, conv_taps, conv_bias):
        return causal_conv(values, conv_taps, conv_bias, segment)

    conv_out, conv_pull = jax.vjp(
        conv_piece, projected[:, :width], temporal_float[:, 0:4], temporal_float[:, 4]
    )
    conv_low = conv_out.astype(brain)
    blocks = conv_low.reshape(length, head_count, head_width)
    gate_logits = jnp.einsum(
        "lhk,hkj->lhj",
        blocks,
        gating_full.reshape(head_count, head_width, 2 * head_width),
        preferred_element_type=jnp.float32,
    )

    def mix_piece(logits, branch_logits, conv_values, recur_bias):
        return temporal_mix(logits, branch_logits, conv_values, recur_bias, resets)

    mixed, mix_pull = jax.vjp(
        mix_piece,
        gate_logits,
        projected[:, width:],
        conv_low.astype(jnp.float32),
        temporal_float[:, 5:8],
    )
    mixed_low = mixed.astype(brain)
    middle = inputs + jnp.dot(mixed_low, contract_full, preferred_element_type=jnp.float32)
    normed_two, norm_two_pull = jax.vjp(rms_scale, middle, scales_float[:, 1])
    normed_two_low = normed_two.astype(brain)
    widened = jnp.dot(normed_two_low, widen_full, preferred_element_type=jnp.float32)

    def gated_piece(values):
        return jax.nn.gelu(values[:, :hidden]) * values[:, hidden:]

    activated, gated_pull = jax.vjp(gated_piece, widened)
    activated_low = activated.astype(brain)
    block_out = (
        middle + jnp.dot(activated_low, narrow_full, preferred_element_type=jnp.float32)
    ).astype(brain)
    upstream = cotangent[0]
    narrow_grad = product_rows(activated_low, upstream)
    activated_grad = product_cols(upstream, narrow_full)
    widened_grad = gated_pull(activated_grad)[0].astype(brain)
    widen_grad = product_rows(normed_two_low, widened_grad)
    normed_two_grad = product_cols(widened_grad, widen_full)
    middle_norm_grad, scale_two_grad = norm_two_pull(normed_two_grad)
    middle_grad = upstream.astype(jnp.float32) + middle_norm_grad
    middle_low = middle_grad.astype(brain)
    contract_grad = product_rows(mixed_low, middle_low)
    mixed_grad = product_cols(middle_low, contract_full)
    logit_grad, branch_grad, conv_mix_grad, recur_bias_grad = mix_pull(mixed_grad)
    logit_low = logit_grad.astype(brain)
    gating_blocks = gating_full.reshape(head_count, head_width, 2 * head_width)
    gating_grad = jnp.einsum(
        "lhk,lhj->hkj", blocks, logit_low, preferred_element_type=jnp.float32
    ).reshape(width, 2 * head_width)
    conv_grad = conv_mix_grad + jnp.einsum(
        "lhj,hkj->lhk", logit_low, gating_blocks, preferred_element_type=jnp.float32
    ).reshape(length, width)
    input_grad, taps_grad, conv_bias_grad = conv_pull(conv_grad)
    projected_low = jnp.concatenate([input_grad, branch_grad], axis=1).astype(brain)
    expand_grad = product_rows(normed_low, projected_low)
    normed_grad = product_cols(projected_low, expand_full)
    token_norm_grad, scale_one_grad = norm_pull(normed_grad)
    tokens_grad = (middle_grad + token_norm_grad).astype(brain)
    scales_grad = jnp.stack([scale_one_grad, scale_two_grad], axis=1)
    temporal_grad = jnp.concatenate([taps_grad, conv_bias_grad[:, None], recur_bias_grad], axis=1)
    devices = 1 << cube.bits
    misc = jnp.concatenate(
        [
            temporal_grad.T.reshape(8, devices, rows_t),
            jnp.pad(scales_grad.T, ((0, 6), (0, 0))).reshape(8, devices, rows_s),
        ],
        axis=2,
    )
    misc = jnp.pad(misc, ((0, 0), (0, 0), (0, 128 - rows_t - rows_s)))
    misc = misc.transpose(1, 0, 2).reshape(devices * 8, 128)
    matrices = (expand_grad, gating_grad, contract_grad, widen_grad, narrow_grad)
    sums, norm_tile = scatter_grads(cube, misc, [g.astype(brain) for g in matrices])
    grads = list(sums[1:]) + [sums[0][:2, rows_t : rows_t + rows_s].T, sums[0][:, :rows_t].T]
    outs = adam_all(
        norm_tile,
        grads,
        (expand, gating, contract, widen, narrow, scales, temporal),
        (expand_mean, gating_mean, contract_mean, widen_mean, narrow_mean, scales_mean, temporal_mean),
        (
            expand_square,
            gating_square,
            contract_square,
            widen_square,
            narrow_square,
            scales_square,
            temporal_square,
        ),
    )
    grad_norm, outs = outs[0][0, 0], outs[1:]
    updated = [outs[i + 7 * j] for i in (0, 2, 1, 3, 4, 5, 6) for j in range(3)]
    return (block_out[None], tokens_grad[None], grad_norm, *updated)


def solution(mesh):
    placed = (
        P(("dp", "fsdp"), None, None),
        P(("dp", "fsdp"), None, None),
        P(("dp", "fsdp"), None),
        P(("dp", "fsdp"), None),
        P(("dp", "fsdp"), None),
        P(("dp", "fsdp"), None),
        P(("dp", "fsdp"), None),
        P(("dp", "fsdp"), None),
        P(("dp", "fsdp"), None),
        P(("dp", "fsdp"), None),
        P(("dp", "fsdp"), None),
        P(("dp", "fsdp"), None),
        P(("dp", "fsdp"), None),
        P(("dp", "fsdp"), None),
        P(("dp", "fsdp"), None),
        P(("dp", "fsdp"), None),
        P(("dp", "fsdp"), None),
        P(("dp", "fsdp"), None),
        P(("dp", "fsdp"), None),
        P(("dp", "fsdp"), None),
        P(("dp", "fsdp"), None),
        P(("dp", "fsdp"), None),
        P(("dp", "fsdp"), None),
        P(("dp", "fsdp"), None),
    )
    return jax.shard_map(
        functools.partial(shards, Cube(mesh.shape)),
        mesh=mesh,
        in_specs=placed,
        out_specs=(
            P(("dp", "fsdp"), None, None),
            P(("dp", "fsdp"), None, None),
            P(),
            P(("dp", "fsdp"), None),
            P(("dp", "fsdp"), None),
            P(("dp", "fsdp"), None),
            P(("dp", "fsdp"), None),
            P(("dp", "fsdp"), None),
            P(("dp", "fsdp"), None),
            P(("dp", "fsdp"), None),
            P(("dp", "fsdp"), None),
            P(("dp", "fsdp"), None),
            P(("dp", "fsdp"), None),
            P(("dp", "fsdp"), None),
            P(("dp", "fsdp"), None),
            P(("dp", "fsdp"), None),
            P(("dp", "fsdp"), None),
            P(("dp", "fsdp"), None),
            P(("dp", "fsdp"), None),
            P(("dp", "fsdp"), None),
            P(("dp", "fsdp"), None),
            P(("dp", "fsdp"), None),
            P(("dp", "fsdp"), None),
            P(("dp", "fsdp"), None),
        ),
        check_vma=False,
    )
```

```python
import functools

import jax
import jax.numpy as jnp
from jax import lax
from jax.experimental import pallas as pl
from jax.experimental.pallas import tpu as pltpu
from jax.sharding import PartitionSpec as P

STEP = 10


NORM_EPSILON = 1e-06
GATE_POWER = 8.0
BETA_FIRST = 0.9
BETA_SECOND = 0.95
ADAM_EPSILON = 1e-08
RATE_MATRIX = 0.1
RATE_VECTOR = 1.0
WEIGHT_DECAY = 0.1
CLIP_NORM = 1.0


MESH = pl.DeviceIdType.MESH
BRAIN = jnp.bfloat16
VMEM_BYTES = 60 * 1024 * 1024


def bit_count(size):
    return size.bit_length() - 1


class Cube:
    def __init__(self, mesh_shape):
        self.dp = bit_count(mesh_shape["dp"])
        self.fsdp = bit_count(mesh_shape["fsdp"])
        self.bits = self.dp + self.fsdp
        self.core = self.dp - 1

    def place(self):
        outer, inner = lax.axis_index("dp"), lax.axis_index("fsdp")
        bits = [lax.rem(outer // (1 << (self.dp - 1 - i)), 2) for i in range(self.dp)]
        return bits + [lax.rem(inner // (1 << (self.fsdp - 1 - i)), 2) for i in range(self.fsdp)]

    def partner(self, place, bit):
        outer, inner = lax.axis_index("dp"), lax.axis_index("fsdp")
        flip = 1 - 2 * place[bit]
        if bit < self.dp:
            return (outer + flip * (1 << (self.dp - 1 - bit)), inner)
        return (outer, inner + flip * (1 << (self.bits - 1 - bit)))

    def orders(self):
        rest = [i for i in range(self.bits) if i != self.core]
        last = rest[-1]
        across = rest[-2]
        lines = rest[:-2]
        return [
            [last] + lines + [across, self.core],
            [across] + lines + [last, self.core],
            lines + [across, last, self.core],
            lines + [last, across, self.core],
        ]


def greet(cube, place):
    barrier = pltpu.get_barrier_semaphore()
    for bit in range(cube.bits):
        pl.semaphore_signal(barrier, inc=1, device_id=cube.partner(place, bit), device_id_type=MESH)
    pl.semaphore_wait(barrier, cube.bits)


def cut_pieces(cube, widths, groups):
    orders = cube.orders()
    pieces = []
    for array, width in enumerate(widths):
        first = 0
        for group, share in groups[array]:
            for columns, order in zip(share, orders):
                if columns:
                    pieces.append((group, array, first, columns * 128, order))
                    first += columns * 128
        assert first == width
    return sorted(pieces, key=lambda piece: piece[0])


def gather_kernel(cube, pieces, count, *refs):
    sources, fulls = refs[:count], refs[count : 2 * count]
    held, own_sem, send_sem, recv_sem = (
        refs[2 * count : 3 * count],
        refs[3 * count],
        refs[3 * count + 1],
        refs[3 * count + 2],
    )
    place = cube.place()
    greet(cube, place)
    own = []
    for i in range(count):
        held[i][...] = sources[i][...].astype(held[i].dtype)
        copy = pltpu.make_async_copy(held[i], fulls[i].at[tuple(place)], own_sem.at[i])
        copy.start()
        own.append(copy)
    for copy in own:
        copy.wait()

    def exchange(number, stage):
        _, array, first, columns, order = pieces[number]
        spot = tuple(
            slice(None) if bit in order[:stage] else place[bit] for bit in range(cube.bits)
        )
        view = fulls[array].at[spot + (slice(None), pl.ds(first, columns))]
        return pltpu.make_async_remote_copy(
            src_ref=view,
            dst_ref=view,
            send_sem=send_sem.at[number, stage],
            recv_sem=recv_sem.at[number, stage],
            device_id=cube.partner(place, order[stage]),
            device_id_type=MESH,
        )

    for slot in range(pieces[-1][0] + cube.bits + 1):
        for number in range(len(pieces)):
            stage = slot - pieces[number][0]
            if 0 <= stage <= cube.bits:
                if stage > 0:
                    exchange(number, stage - 1).wait_recv()
                if stage < cube.bits:
                    exchange(number, stage).start()
    for number in range(len(pieces)):
        for stage in range(cube.bits):
            exchange(number, stage).wait_send()


def gather_all(cube, shards_in, kinds, groups):
    count = len(shards_in)
    pieces = cut_pieces(cube, [s.shape[1] for s in shards_in], groups)
    fulls = [(2,) * cube.bits + s.shape for s in shards_in]
    gathered = pl.pallas_call(
        functools.partial(gather_kernel, cube, pieces, count),
        out_shape=[jax.ShapeDtypeStruct(shape, kind) for shape, kind in zip(fulls, kinds)],
        in_specs=[pl.BlockSpec(memory_space=pltpu.VMEM)] * count,
        out_specs=[pl.BlockSpec(memory_space=pl.ANY)] * count,
        scratch_shapes=[pltpu.VMEM(s.shape, kind) for s, kind in zip(shards_in, kinds)]
        + [
            pltpu.SemaphoreType.DMA((count,)),
            pltpu.SemaphoreType.DMA((len(pieces), cube.bits)),
            pltpu.SemaphoreType.DMA((len(pieces), cube.bits)),
        ],
        compiler_params=pltpu.CompilerParams(
            collective_id=0, has_side_effects=True, vmem_limit_bytes=VMEM_BYTES
        ),
    )(*shards_in)
    return [g.reshape((-1,) + g.shape[cube.bits + 1 :]) for g in gathered]


def scatter_kernel(cube, pieces, count, *refs):
    grads, sums = refs[:count], refs[count : 2 * count]
    norm = refs[2 * count]
    refs = refs[2 * count + 1 :]
    held = refs[:count]
    inbox = [
        refs[(1 + stage) * count : (2 + stage) * count] for stage in range(cube.bits)
    ]
    own_sem, send_sem, recv_sem, partial, other, norm_send, norm_recv = refs[
        (1 + cube.bits) * count :
    ]
    place = cube.place()
    greet(cube, place)

    def bits_left(number, stage):
        order = pieces[number][4]
        return [bit for bit in range(cube.bits) if bit not in order[cube.bits - stage :]]

    def own_copy(number):
        _, array, first, columns, order = pieces[number]
        spot = tuple(place[bit] if bit == order[-1] else slice(None) for bit in range(cube.bits))
        window = (slice(None), pl.ds(first, columns))
        rest = (slice(None),) * (cube.bits - 1)
        return pltpu.make_async_copy(
            grads[array].at[spot + window], held[array].at[rest + window], own_sem.at[number]
        )

    def exchange(number, stage):
        _, array, first, columns, order = pieces[number]
        bit = order[cube.bits - 1 - stage]
        left = bits_left(number, stage)
        source = grads[array] if stage == 0 else inbox[stage - 1][array]
        spot = tuple(1 - place[bit] if b == bit else slice(None) for b in left)
        window = (slice(None), pl.ds(first, columns))
        rest = (slice(None),) * (len(left) - 1)
        return pltpu.make_async_remote_copy(
            src_ref=source.at[spot + window],
            dst_ref=inbox[stage][array].at[rest + window],
            send_sem=send_sem.at[number, stage],
            recv_sem=recv_sem.at[number, stage],
            device_id=cube.partner(place, bit),
            device_id_type=MESH,
        )

    def add(number, stage):
        _, array, first, columns, order = pieces[number]
        bit = order[cube.bits - 1 - stage]
        left = bits_left(number, stage)
        after = [b for b in left if b != bit]
        window = (slice(None), pl.ds(first, columns))
        target = inbox[stage][array]

        def one(step, carry):
            spot = tuple(
                lax.rem(step // (1 << (len(after) - 1 - i)), 2) for i in range(len(after))
            )
            if stage == 0:
                mine = held[array][spot + window]
            else:
                mixed = list(spot)
                mixed.insert(left.index(bit), place[bit])
                mine = inbox[stage - 1][array][tuple(mixed) + window]
            total = mine.astype(jnp.float32) + target[spot + window].astype(jnp.float32)
            if stage == cube.bits - 1:
                sums[array][window] = total
                squares = total * total
                tile = squares.reshape(squares.shape[0] // 8, 8, columns).sum(axis=0)
                for start in range(0, columns, 128):
                    partial[0] += tile[:, start : start + 128]
            else:
                target[spot + window] = total.astype(target.dtype)
            return carry

        lax.fori_loop(0, 1 << len(after), one, 0)

    partial[0] = jnp.zeros(partial.shape[1:], jnp.float32)
    for number in range(len(pieces)):
        own_copy(number).start()
    for slot in range(pieces[-1][0] + cube.bits + 1):
        for number in range(len(pieces)):
            stage = slot - pieces[number][0]
            if 0 <= stage <= cube.bits:
                if stage > 0:
                    if stage == 1:
                        own_copy(number).wait()
                    exchange(number, stage - 1).wait_recv()
                    add(number, stage - 1)
                if stage < cube.bits:
                    exchange(number, stage).start()
    for number in range(len(pieces)):
        for stage in range(cube.bits):
            exchange(number, stage).wait_send()
    for bit in range(cube.bits):
        copy = pltpu.make_async_remote_copy(
            src_ref=partial.at[bit],
            dst_ref=other.at[bit],
            send_sem=norm_send.at[bit],
            recv_sem=norm_recv.at[bit],
            device_id=cube.partner(place, bit),
            device_id_type=MESH,
        )
        copy.start()
        copy.wait()
        if bit < cube.bits - 1:
            partial[bit + 1] = partial[bit] + other[bit]
        else:
            norm[...] = partial[bit] + other[bit]


def scatter_all(cube, grads, groups):
    count = len(grads)
    devices = 1 << cube.bits
    shapes = [(g.shape[0] // devices, g.shape[1]) for g in grads]
    pieces = cut_pieces(cube, [g.shape[1] for g in grads], groups)
    scratch = [
        pltpu.VMEM((2,) * (cube.bits - 1) + shape, g.dtype) for shape, g in zip(shapes, grads)
    ]
    for stage in range(cube.bits):
        scratch += [
            pltpu.VMEM((2,) * (cube.bits - 1 - stage) + shape, g.dtype)
            for shape, g in zip(shapes, grads)
        ]
    return pl.pallas_call(
        functools.partial(scatter_kernel, cube, pieces, count),
        out_shape=[jax.ShapeDtypeStruct(shape, jnp.float32) for shape in shapes + [(8, 128)]],
        in_specs=[pl.BlockSpec(memory_space=pl.ANY)] * count,
        out_specs=[pl.BlockSpec(memory_space=pltpu.VMEM)] * (count + 1),
        scratch_shapes=scratch
        + [
            pltpu.SemaphoreType.DMA((len(pieces),)),
            pltpu.SemaphoreType.DMA((len(pieces), cube.bits)),
            pltpu.SemaphoreType.DMA((len(pieces), cube.bits)),
            pltpu.VMEM((cube.bits, 8, 128), jnp.float32),
            pltpu.VMEM((cube.bits, 8, 128), jnp.float32),
            pltpu.SemaphoreType.DMA((cube.bits,)),
            pltpu.SemaphoreType.DMA((cube.bits,)),
        ],
        compiler_params=pltpu.CompilerParams(
            collective_id=1, has_side_effects=True, vmem_limit_bytes=VMEM_BYTES
        ),
    )(*[g.reshape((2,) * cube.bits + s) for g, s in zip(grads, shapes)])


GROUPS = (
    ((0, (0, 0, 1, 0)),),
    ((0, (2, 2, 4, 4)), (1, (2, 2, 4, 4))),
    ((2, (0, 0, 1, 1)),),
    ((2, (1, 1, 3, 3)),),
    ((3, (2, 2, 4, 4)), (4, (2, 2, 4, 4)), (5, (2, 2, 4, 4)), (6, (2, 2, 4, 4))),
    ((7, (1, 1, 1, 1)), (8, (1, 1, 1, 1))),
)
AXES = ("dp", "fsdp")


def pack_vectors(temporal, scales):
    upper = jnp.concatenate([temporal.T, jnp.pad(scales.T, ((0, 6), (0, 0)))], axis=1)
    return jnp.pad(upper, ((0, 0), (0, 128 - upper.shape[1])))


def gather_params(cube, misc, matrices):
    if all(m.shape[0] % 16 == 0 for m in matrices):
        kinds = [jnp.float32] + [BRAIN] * len(matrices)
        return gather_all(cube, [misc] + list(matrices), kinds, GROUPS)
    sent = [misc] + [m.astype(BRAIN) for m in matrices]
    return [lax.all_gather(v, AXES, axis=0, tiled=True) for v in sent]


def scatter_grads(cube, misc, grads):
    if all((g.shape[0] >> cube.bits) % 16 == 0 for g in grads):
        outs = scatter_all(cube, [misc] + list(grads), GROUPS)
        return outs[:-1], outs[-1]
    sums = [
        lax.psum_scatter(g.astype(jnp.float32), AXES, scatter_dimension=0, tiled=True)
        for g in [misc] + list(grads)
    ]
    squares = lax.psum(sum(jnp.sum(s * s) for s in sums), AXES)
    return sums, jnp.pad(squares[None, None], ((0, 7), (0, 127)))


def adam_kernel(count, norm_tile, *refs):
    grads, olds, ones, twos = (refs[i * count : (i + 1) * count] for i in range(4))
    norm_ref = refs[4 * count]
    afters, new_ones, new_twos = (
        refs[4 * count + 1 + i * count : 4 * count + 1 + (i + 1) * count] for i in range(3)
    )
    grad_norm = jnp.sqrt(jnp.sum(norm_tile[...], keepdims=True))
    norm_ref[...] = grad_norm
    factor = CLIP_NORM / jnp.maximum(grad_norm, CLIP_NORM)
    for i in range(count):
        matrix = i < count - 2
        after, one, two = adam_update(
            olds[i][...],
            ones[i][...],
            twos[i][...],
            grads[i][...],
            factor,
            RATE_MATRIX if matrix else RATE_VECTOR,
            WEIGHT_DECAY if matrix else 0.0,
        )
        afters[i][...] = after
        new_ones[i][...] = one
        new_twos[i][...] = two


def adam_all(norm_tile, grads, olds, ones, twos):
    count = len(grads)
    like = [jax.ShapeDtypeStruct(v.shape, v.dtype) for v in olds]
    return pl.pallas_call(
        functools.partial(adam_kernel, count),
        out_shape=[jax.ShapeDtypeStruct((1, 1), jnp.float32)] + like * 3,
        compiler_params=pltpu.CompilerParams(vmem_limit_bytes=VMEM_BYTES),
    )(norm_tile, *grads, *olds, *ones, *twos)


GELU_ONE = 0.7978845608028654
GELU_THREE = GELU_ONE * 0.044715
LANES = 128
ROWS = 8


def sigmoid(v):
    return 0.5 * jnp.tanh(0.5 * v) + 0.5


def gelu_parts(v):
    square = v * v
    turned = jnp.tanh(v * (GELU_ONE + GELU_THREE * square))
    half = 0.5 * turned + 0.5
    slope = half + (0.5 * v) * (1.0 - turned * turned) * (GELU_ONE + (3.0 * GELU_THREE) * square)
    return half, slope


def gelu_half(v):
    return 0.5 * jnp.tanh(v * (GELU_ONE + GELU_THREE * (v * v))) + 0.5


def one_less_exp(v, exp_v):
    series = 1.0 + v * (1.0 / 7.0)
    for order in (6.0, 5.0, 4.0, 3.0, 2.0):
        series = 1.0 + v * (1.0 / order) * series
    return jnp.where(v > -0.35, -v * series, 1.0 - exp_v)


def row_mask(width, first, last):
    rows = lax.broadcasted_iota(jnp.int32, (ROWS, width), 0)
    return (rows >= first) & (rows < last)


def shifted_down(now, before, steps, mask):
    return jnp.where(mask, pltpu.roll(now, steps, 0), pltpu.roll(before, steps, 0))


def shifted_up(now, after, steps, mask):
    return jnp.where(mask, pltpu.roll(now, ROWS - steps, 0), pltpu.roll(after, ROWS - steps, 0))


def wide(column, width):
    return column if width == LANES else jnp.concatenate([column] * (width // LANES), axis=1)


def rms_rows(source, gain, target, places):
    def one(tile, carry):
        rows = pl.ds(pl.multiple_of(tile * 16, 16), 16)
        v = source[rows, :].astype(jnp.float32)
        scale = lax.rsqrt(jnp.mean(v * v, axis=-1, keepdims=True) + NORM_EPSILON)
        target[rows, :] = (v * scale * gain[...]).astype(target.dtype)
        return carry

    lax.fori_loop(0, places // 16, one, 0, unroll=2)


def conv_forward(u, vec, masks, conv, lanes, width, places):
    taps = [jnp.broadcast_to(vec[k : k + 1, lanes], (ROWS, width)) for k in range(5)]
    inside = [row_mask(width, k, ROWS) for k in range(4)]

    def one(tile, before):
        parts = []
        for half in range(2):
            rows = pl.ds(pl.multiple_of(tile * 16 + half * 8, 8), ROWS)
            now = u[rows, lanes]
            total = taps[4] + now * taps[0]
            for k in range(1, 4):
                keep = wide(masks[k - 1, rows, :], width)
                total = total + shifted_down(now, before, k, inside[k]) * taps[k] * keep
            parts.append(total)
            before = now
        rows = pl.ds(pl.multiple_of(tile * 16, 16), 16)
        conv[rows, lanes] = jnp.concatenate(parts, axis=0).astype(conv.dtype)
        return before

    lax.fori_loop(0, places // 16, one, jnp.zeros((ROWS, width), jnp.float32), unroll=2)


def scan_tile(decay, value, masks, sign):
    for steps, mask in zip((1, 2, 4), masks):
        turn = steps if sign > 0 else ROWS - steps
        value = value + decay * jnp.where(mask, pltpu.roll(value, turn, 0), 0.0)
        decay = decay * jnp.where(mask, pltpu.roll(decay, turn, 0), 1.0)
    return decay, value


def mix_forward(recur, inlet, branch, conv, vec, masks, state, mixed, lanes, width, places):
    bias_r = jnp.broadcast_to(vec[5:6, lanes], (ROWS, width))
    bias_i = jnp.broadcast_to(vec[6:7, lanes], (ROWS, width))
    power = jnp.broadcast_to(vec[8:9, lanes], (ROWS, width))
    inside = [row_mask(width, k, ROWS) for k in (1, 2, 4)]

    def one(tile, carry):
        low_rows = pl.ds(pl.multiple_of(tile * 16, 16), 16)
        convs = conv[low_rows, lanes].astype(jnp.float32)
        parts = []
        for half in range(2):
            rows = pl.ds(pl.multiple_of(tile * 16 + half * 8, 8), ROWS)
            going = wide(masks[0, rows, :], width)
            gate_r = sigmoid(recur[rows, lanes] + bias_r)
            gate_i = sigmoid(inlet[rows, lanes] + bias_i)
            recur[rows, lanes] = gate_r
            inlet[rows, lanes] = gate_i
            log_decay = gate_r * power
            decay = jnp.exp(log_decay)
            scaling = jnp.sqrt(one_less_exp(2.0 * log_decay, decay * decay))
            scaling = scaling * going + (1.0 - going)
            value = scaling * gate_i * convs[half * 8 : half * 8 + 8]
            span, value = scan_tile(decay * going, value, inside, 1)
            value = value + span * carry
            carry = jnp.broadcast_to(value[ROWS - 1 : ROWS, :], (ROWS, width))
            state[rows, lanes] = value
            gate_b = branch[rows, lanes]
            parts.append(value * (gate_b * gelu_half(gate_b)))
        mixed[low_rows, lanes] = jnp.concatenate(parts, axis=0).astype(mixed.dtype)
        return carry

    lax.fori_loop(0, places // 16, one, jnp.zeros((ROWS, width), jnp.float32), unroll=2)


def mix_backward(
    grad, recur, inlet, branch, conv, state, vec, masks, low_r, low_i, direct, low_b, tallies, lanes, width, places
):
    power = jnp.broadcast_to(vec[8:9, lanes], (ROWS, width))
    below = [row_mask(width, 0, ROWS - k) for k in (1, 2, 4)]
    first = row_mask(width, 1, ROWS)
    tiles = places // 16
    nothing = jnp.zeros((ROWS, width), jnp.float32)

    def one(step, carries):
        carry, after, sum_r, sum_i, sum_p = carries
        tile = tiles - 1 - step
        low_rows = pl.ds(pl.multiple_of(tile * 16, 16), 16)
        convs = conv[low_rows, lanes].astype(jnp.float32)
        outs = [[None, None] for _ in range(4)]
        for half in (1, 0):
            at = tile * 16 + half * 8
            rows = pl.ds(pl.multiple_of(at, 8), ROWS)
            going = wide(masks[0, rows, :], width)
            gate_r, gate_i = recur[rows, lanes], inlet[rows, lanes]
            values = convs[half * 8 : half * 8 + 8]
            now = state[rows, lanes]
            earlier = state[pl.ds(pl.multiple_of(jnp.maximum(at - 8, 0), 8), ROWS), lanes]
            last = shifted_down(now, earlier, 1, first)
            log_decay = gate_r * power
            plain = jnp.exp(log_decay)
            square = plain * plain
            lost = one_less_exp(2.0 * log_decay, square)
            inverse = lax.rsqrt(lost)
            scaling = (lost * inverse) * going + (1.0 - going)
            gate_b = branch[rows, lanes]
            half_b, slope_b = gelu_parts(gate_b)
            mixed_grad = grad[rows, lanes]
            decay = plain * going
            later = shifted_up(decay, after, 1, below[0])
            span, total = scan_tile(later, mixed_grad * (gate_b * half_b), below, -1)
            total = total + span * carry
            carry = jnp.broadcast_to(total[0:1, :], (ROWS, width))
            after = decay
            outs[3][half] = mixed_grad * now * slope_b
            scaled = total * scaling
            flow = total * gate_i
            outs[2][half] = scaled * gate_i
            grad_i = scaled * values * (gate_i * (1.0 - gate_i))
            log_grad = going * (total * last * plain - flow * values * (square * inverse))
            grad_p = gate_r * log_grad
            grad_r = grad_p * ((1.0 - gate_r) * power)
            outs[0][half], outs[1][half] = grad_r, grad_i
            sum_r, sum_i, sum_p = sum_r + grad_r, sum_i + grad_i, sum_p + grad_p
        for target, parts in zip((low_r, low_i, direct, low_b), outs):
            target[low_rows, lanes] = jnp.concatenate(parts, axis=0).astype(target.dtype)
        return carry, after, sum_r, sum_i, sum_p

    sums = lax.fori_loop(0, tiles, one, (nothing,) * 5, unroll=2)[2:]
    tallies[5:6, lanes] = jnp.sum(sums[0], axis=0, keepdims=True)
    tallies[6:7, lanes] = jnp.sum(sums[1], axis=0, keepdims=True)
    tallies[7:8, lanes] = jnp.sum(sums[2], axis=0, keepdims=True) * vec[9:10, lanes]


def conv_backward(direct, u, vec, masks, low_u, tallies, lanes, width, places):
    taps = [jnp.broadcast_to(vec[k : k + 1, lanes], (ROWS, width)) for k in range(4)]
    inside = [row_mask(width, k, ROWS) for k in range(4)]
    below = [row_mask(width, 0, ROWS - k) for k in range(4)]
    tiles = places // 16
    nothing = jnp.zeros((ROWS, width), jnp.float32)

    def one(step, carries):
        afters, sums = list(carries[:3]), list(carries[3:])
        tile = tiles - 1 - step
        parts = [None, None]
        for half in (1, 0):
            at = tile * 16 + half * 8
            rows = pl.ds(pl.multiple_of(at, 8), ROWS)
            grad = direct[rows, lanes]
            now = u[rows, lanes]
            earlier = u[pl.ds(pl.multiple_of(jnp.maximum(at - 8, 0), 8), ROWS), lanes]
            total = grad * taps[0]
            sums[0] = sums[0] + grad * now
            sums[4] = sums[4] + grad
            for k in range(1, 4):
                kept = grad * wide(masks[k - 1, rows, :], width)
                total = total + taps[k] * shifted_up(kept, afters[k - 1], k, below[k])
                sums[k] = sums[k] + kept * shifted_down(now, earlier, k, inside[k])
                afters[k - 1] = kept
            parts[half] = total
        low_rows = pl.ds(pl.multiple_of(tile * 16, 16), 16)
        low_u[low_rows, lanes] = jnp.concatenate(parts, axis=0).astype(low_u.dtype)
        return (*afters, *sums)

    sums = lax.fori_loop(0, tiles, one, (nothing,) * 8, unroll=2)[3:]
    for k in range(5):
        tallies[k : k + 1, lanes] = jnp.sum(sums[k], axis=0, keepdims=True)


def product_into(target, lanes, first, second, pieces, extra=None):
    rows_in = first.shape[0] // pieces

    def one(piece, carry):
        rows = pl.ds(pl.multiple_of(piece * rows_in, rows_in), rows_in)
        total = jnp.dot(first[rows, :], second, preferred_element_type=jnp.float32)
        if extra is not None:
            total = total + extra[rows, lanes].astype(jnp.float32)
        target[rows, lanes] = total.astype(target.dtype)
        return carry

    lax.fori_loop(0, pieces, one, 0)


def mixer_forward_kernel(
    width, tokens, gain_one, gain_two, vec, masks, expand, gating, contract,
    normed, u, branch, recur, inlet, conv, state, mixed, middle, normed_two,
):
    places, channels = u.shape
    head = gating.shape[1] // 2
    rms_rows(tokens, gain_one, normed, places)

    def group(index, carry):
        lanes = pl.ds(pl.multiple_of(index * width, width), width)
        right = pl.ds(pl.multiple_of(channels + index * width, width), width)
        product_into(u, lanes, normed, expand[:, lanes], 2)
        product_into(branch, lanes, normed, expand[:, right], 2)
        conv_forward(u, vec, masks, conv, lanes, width, places)
        for part in range(width // head):
            spot = pl.ds(pl.multiple_of(index * width + part * head, head), head)
            logits = jnp.dot(conv[:, spot], gating[spot, :], preferred_element_type=jnp.float32)
            recur[:, spot] = logits[:, :head]
            inlet[:, spot] = logits[:, head:]
        mix_forward(recur, inlet, branch, conv, vec, masks, state, mixed, lanes, width, places)
        return carry

    lax.fori_loop(0, channels // width, group, 0)

    def column(index, carry):
        lanes = pl.ds(pl.multiple_of(index * 256, 256), 256)
        product_into(middle, lanes, mixed, contract[:, lanes], 2, tokens)
        return carry

    lax.fori_loop(0, middle.shape[1] // 256, column, 0)
    rms_rows(middle, gain_two, normed_two, places)


def mixer_forward(tokens, gain_one, gain_two, vec, masks, expand, gating, contract, width=256):
    places, features = tokens.shape
    channels = contract.shape[0]
    wide_f32 = jax.ShapeDtypeStruct((places, channels), jnp.float32)
    wide_low = jax.ShapeDtypeStruct((places, channels), BRAIN)
    return pl.pallas_call(
        functools.partial(mixer_forward_kernel, width),
        out_shape=[
            jax.ShapeDtypeStruct((places, features), BRAIN),
            wide_f32, wide_f32, wide_f32, wide_f32, wide_low, wide_f32, wide_low,
            jax.ShapeDtypeStruct((places, features), jnp.float32),
            jax.ShapeDtypeStruct((places, features), BRAIN),
        ],
        compiler_params=pltpu.CompilerParams(vmem_limit_bytes=VMEM_BYTES),
    )(tokens, gain_one, gain_two, vec, masks, expand, gating, contract)


def mixer_backward_kernel(
    width, low, contract, gating, vec, masks, u, branch, recur, inlet, conv, state,
    low_p, gating_grad, tallies, grad, direct, low_r, low_i,
):
    places, channels = u.shape
    head = gating.shape[1] // 2

    def group(index, carry):
        lanes = pl.ds(pl.multiple_of(index * width, width), width)
        right = pl.ds(pl.multiple_of(channels + index * width, width), width)
        total = lax.dot_general(
            low[...], contract[lanes, :], (((1,), (1,)), ((), ())), preferred_element_type=jnp.float32
        )
        grad[...] = total
        here = slice(0, width)
        views = [v.at[:, lanes] for v in (recur, inlet, branch, conv, state)]
        mix_backward(
            grad, *views, vec.at[:, lanes], masks, low_r, low_i, direct,
            low_p.at[:, right], tallies.at[:, lanes], here, width, places,
        )
        for part in range(width // head):
            spot = slice(part * head, (part + 1) * head)
            at = pl.ds(pl.multiple_of(index * width + part * head, head), head)
            low_both = jnp.concatenate([low_r[:, spot], low_i[:, spot]], axis=1)
            gating_grad[at, :] = lax.dot_general(
                conv[:, at], low_both, (((0,), (0,)), ((), ())), preferred_element_type=jnp.float32
            ).astype(gating_grad.dtype)
            direct[:, spot] += lax.dot_general(
                low_both, gating[at, :], (((1,), (1,)), ((), ())), preferred_element_type=jnp.float32
            )
        conv_backward(
            direct, u.at[:, lanes], vec.at[:, lanes], masks, low_p.at[:, lanes], tallies.at[:, lanes],
            here, width, places,
        )
        return carry

    lax.fori_loop(0, channels // width, group, 0)


def mixer_backward(low, contract, gating, vec, masks, u, branch, recur, inlet, conv, state, width=256):
    places, channels = u.shape
    return pl.pallas_call(
        functools.partial(mixer_backward_kernel, width),
        out_shape=[
            jax.ShapeDtypeStruct((places, 2 * channels), BRAIN),
            jax.ShapeDtypeStruct(gating.shape, BRAIN),
            jax.ShapeDtypeStruct((8, channels), jnp.float32),
        ],
        scratch_shapes=[
            pltpu.VMEM((places, width), jnp.float32),
            pltpu.VMEM((places, width), jnp.float32),
            pltpu.VMEM((places, width), BRAIN),
            pltpu.VMEM((places, width), BRAIN),
        ],
        compiler_params=pltpu.CompilerParams(vmem_limit_bytes=VMEM_BYTES),
    )(low, contract, gating, vec, masks, u, branch, recur, inlet, conv, state)


def channel_rows(temporal_rows):
    decay = temporal_rows[7:8]
    power = -GATE_POWER * jax.nn.softplus(-decay)
    slope = GATE_POWER * jax.nn.sigmoid(-decay)
    return jnp.concatenate([temporal_rows, power, slope, jnp.zeros_like(temporal_rows)[:6]], axis=0)


def keep_masks(lengths, length):
    starts = jnp.cumsum(lengths) - lengths
    places = jnp.arange(length, dtype=jnp.int32)
    resets = jnp.any(places[:, None] == starts[None, :], axis=-1)
    one = 1.0 - resets.astype(jnp.float32)
    two = one * jnp.concatenate([jnp.zeros((1,)), one[:-1]])
    three = two * jnp.concatenate([jnp.zeros((2,)), one[:-2]])
    return jnp.broadcast_to(jnp.stack([one, two, three])[:, :, None], (3, length, LANES))


def rms_pull(values, gain, grad):
    scale = lax.rsqrt(jnp.mean(values * values, axis=-1, keepdims=True) + NORM_EPSILON)
    scaled = grad * gain
    inner = jnp.mean(values * scaled, axis=-1, keepdims=True)
    return scale * scaled - values * (scale * scale * scale * inner), jnp.sum(grad * values * scale, axis=0)


def product_rows(former, latter):
    return lax.dot_general(
        former, latter, (((0,), (0,)), ((), ())), preferred_element_type=jnp.float32
    )


def product_cols(former, latter):
    return lax.dot_general(
        former, latter, (((1,), (1,)), ((), ())), preferred_element_type=jnp.float32
    )


def adam_update(master, moment_one, moment_two, gradient, factor, rate, decay):
    clipped = gradient * factor
    new_one = BETA_FIRST * moment_one + (1.0 - BETA_FIRST) * clipped
    new_two = BETA_SECOND * moment_two + (1.0 - BETA_SECOND) * clipped * clipped
    first_hat = new_one / (1.0 - BETA_FIRST**STEP)
    second_hat = new_two / (1.0 - BETA_SECOND**STEP)
    after = master - rate * (first_hat / (jnp.sqrt(second_hat) + ADAM_EPSILON) + decay * master)
    return (after, new_one, new_two)


def shards(
    cube,
    tokens,
    cotangent,
    doc_lengths,
    expand,
    expand_mean,
    expand_square,
    contract,
    contract_mean,
    contract_square,
    gating,
    gating_mean,
    gating_square,
    widen,
    widen_mean,
    widen_square,
    narrow,
    narrow_mean,
    narrow_square,
    scales,
    scales_mean,
    scales_square,
    temporal,
    temporal_mean,
    temporal_square,
):
    brain = jnp.bfloat16
    rows_t, rows_s = temporal.shape[0], scales.shape[0]
    vectors = pack_vectors(temporal, scales).astype(brain).astype(jnp.float32)
    vectors, expand_full, gating_full, contract_full, widen_full, narrow_full = gather_params(
        cube, vectors, (expand, gating, contract, widen, narrow)
    )
    vectors = vectors.reshape(-1, 8, 128).transpose(0, 2, 1)
    temporal_float = vectors[:, :rows_t].reshape(-1, 8)
    scales_float = vectors[:, rows_t : rows_t + rows_s, :2].reshape(-1, 2)
    hidden = narrow_full.shape[0]
    length = tokens.shape[1]
    inputs = tokens[0]
    vec = channel_rows(temporal_float.T)
    masks = keep_masks(doc_lengths[0], length)
    gains = scales_float.T
    normed, u, branch, recur, inlet, conv, state, mixed, middle, normed_two = mixer_forward(
        inputs, gains[0:1], gains[1:2], vec, masks, expand_full, gating_full, contract_full
    )
    widened = jnp.dot(normed_two, widen_full, preferred_element_type=jnp.float32)
    gate, up = widened[:, :hidden], widened[:, hidden:]
    half, slope = gelu_parts(gate)
    activated = (gate * half * up).astype(brain)
    block_out = (
        middle + jnp.dot(activated, narrow_full, preferred_element_type=jnp.float32)
    ).astype(brain)
    upstream = cotangent[0]
    narrow_grad = product_rows(activated, upstream)
    activated_grad = product_cols(upstream, narrow_full)
    widened_grad = jnp.concatenate(
        [activated_grad * up * slope, activated_grad * (gate * half)], axis=1
    ).astype(brain)
    widen_grad = product_rows(normed_two, widened_grad)
    normed_two_grad = product_cols(widened_grad, widen_full)
    middle_norm_grad, scale_two_grad = rms_pull(middle, gains[1], normed_two_grad)
    middle_grad = upstream.astype(jnp.float32) + middle_norm_grad
    middle_low = middle_grad.astype(brain)
    contract_grad = product_rows(mixed, middle_low)
    projected_low, gating_grad, temporal_grad = mixer_backward(
        middle_low, contract_full, gating_full, vec, masks, u, branch, recur, inlet, conv, state
    )
    expand_grad = product_rows(normed, projected_low)
    normed_grad = product_cols(projected_low, expand_full)
    token_norm_grad, scale_one_grad = rms_pull(inputs.astype(jnp.float32), gains[0], normed_grad)
    tokens_grad = (middle_grad + token_norm_grad).astype(brain)
    scales_grad = jnp.stack([scale_one_grad, scale_two_grad])
    devices = 1 << cube.bits
    misc = jnp.concatenate(
        [
            temporal_grad.reshape(8, devices, rows_t),
            jnp.pad(scales_grad, ((0, 6), (0, 0))).reshape(8, devices, rows_s),
        ],
        axis=2,
    )
    misc = jnp.pad(misc, ((0, 0), (0, 0), (0, 128 - rows_t - rows_s)))
    misc = misc.transpose(1, 0, 2).reshape(devices * 8, 128)
    matrices = (expand_grad, gating_grad, contract_grad, widen_grad, narrow_grad)
    sums, norm_tile = scatter_grads(cube, misc, [g.astype(brain) for g in matrices])
    grads = list(sums[1:]) + [sums[0][:2, rows_t : rows_t + rows_s].T, sums[0][:, :rows_t].T]
    outs = adam_all(
        norm_tile,
        grads,
        (expand, gating, contract, widen, narrow, scales, temporal),
        (expand_mean, gating_mean, contract_mean, widen_mean, narrow_mean, scales_mean, temporal_mean),
        (
            expand_square,
            gating_square,
            contract_square,
            widen_square,
            narrow_square,
            scales_square,
            temporal_square,
        ),
    )
    grad_norm, outs = outs[0][0, 0], outs[1:]
    updated = [outs[i + 7 * j] for i in (0, 2, 1, 3, 4, 5, 6) for j in range(3)]
    return (block_out[None], tokens_grad[None], grad_norm, *updated)


def solution(mesh):
    placed = (
        P(("dp", "fsdp"), None, None),
        P(("dp", "fsdp"), None, None),
        P(("dp", "fsdp"), None),
        P(("dp", "fsdp"), None),
        P(("dp", "fsdp"), None),
        P(("dp", "fsdp"), None),
        P(("dp", "fsdp"), None),
        P(("dp", "fsdp"), None),
        P(("dp", "fsdp"), None),
        P(("dp", "fsdp"), None),
        P(("dp", "fsdp"), None),
        P(("dp", "fsdp"), None),
        P(("dp", "fsdp"), None),
        P(("dp", "fsdp"), None),
        P(("dp", "fsdp"), None),
        P(("dp", "fsdp"), None),
        P(("dp", "fsdp"), None),
        P(("dp", "fsdp"), None),
        P(("dp", "fsdp"), None),
        P(("dp", "fsdp"), None),
        P(("dp", "fsdp"), None),
        P(("dp", "fsdp"), None),
        P(("dp", "fsdp"), None),
        P(("dp", "fsdp"), None),
    )
    return jax.shard_map(
        functools.partial(shards, Cube(mesh.shape)),
        mesh=mesh,
        in_specs=placed,
        out_specs=(
            P(("dp", "fsdp"), None, None),
            P(("dp", "fsdp"), None, None),
            P(),
            P(("dp", "fsdp"), None),
            P(("dp", "fsdp"), None),
            P(("dp", "fsdp"), None),
            P(("dp", "fsdp"), None),
            P(("dp", "fsdp"), None),
            P(("dp", "fsdp"), None),
            P(("dp", "fsdp"), None),
            P(("dp", "fsdp"), None),
            P(("dp", "fsdp"), None),
            P(("dp", "fsdp"), None),
            P(("dp", "fsdp"), None),
            P(("dp", "fsdp"), None),
            P(("dp", "fsdp"), None),
            P(("dp", "fsdp"), None),
            P(("dp", "fsdp"), None),
            P(("dp", "fsdp"), None),
            P(("dp", "fsdp"), None),
            P(("dp", "fsdp"), None),
            P(("dp", "fsdp"), None),
            P(("dp", "fsdp"), None),
            P(("dp", "fsdp"), None),
        ),
        check_vma=False,
    )
```

```python
import functools

import jax
import jax.numpy as jnp
from jax import lax
from jax.experimental import pallas as pl
from jax.experimental.pallas import tpu as pltpu
from jax.sharding import PartitionSpec as P

STEP = 10


NORM_EPSILON = 1e-06
GATE_POWER = 8.0
BETA_FIRST = 0.9
BETA_SECOND = 0.95
ADAM_EPSILON = 1e-08
RATE_MATRIX = 0.1
RATE_VECTOR = 1.0
WEIGHT_DECAY = 0.1
CLIP_NORM = 1.0


MESH = pl.DeviceIdType.MESH
BRAIN = jnp.bfloat16
VMEM_BYTES = 60 * 1024 * 1024


def bit_count(size):
    return size.bit_length() - 1


class Cube:
    def __init__(self, mesh_shape):
        self.dp = bit_count(mesh_shape["dp"])
        self.fsdp = bit_count(mesh_shape["fsdp"])
        self.bits = self.dp + self.fsdp
        self.core = self.dp - 1

    def place(self):
        outer, inner = lax.axis_index("dp"), lax.axis_index("fsdp")
        bits = [lax.rem(outer // (1 << (self.dp - 1 - i)), 2) for i in range(self.dp)]
        return bits + [lax.rem(inner // (1 << (self.fsdp - 1 - i)), 2) for i in range(self.fsdp)]

    def partner(self, place, bit):
        outer, inner = lax.axis_index("dp"), lax.axis_index("fsdp")
        flip = 1 - 2 * place[bit]
        if bit < self.dp:
            return (outer + flip * (1 << (self.dp - 1 - bit)), inner)
        return (outer, inner + flip * (1 << (self.bits - 1 - bit)))

    def beyond(self, place, flipped):
        outer, inner = lax.axis_index("dp"), lax.axis_index("fsdp")
        for bit in flipped:
            flip = 1 - 2 * place[bit]
            if bit < self.dp:
                outer = outer + flip * (1 << (self.dp - 1 - bit))
            else:
                inner = inner + flip * (1 << (self.bits - 1 - bit))
        return (outer, inner)

    def circles(self):
        return [list(range(2, self.bits)), [0, 1]]

    def subsets(self, members):
        return [
            [bit for i, bit in enumerate(members) if (number >> i) % 2]
            for number in range(1, 1 << len(members))
        ]

    def orders(self):
        rest = [i for i in range(self.bits) if i != self.core]
        last = rest[-1]
        across = rest[-2]
        lines = rest[:-2]
        return [
            [last] + lines + [across, self.core],
            [across] + lines + [last, self.core],
            lines + [across, last, self.core],
            lines + [last, across, self.core],
        ]


def greet(cube, place, others=None):
    others = [[bit] for bit in range(cube.bits)] if others is None else others
    barrier = pltpu.get_barrier_semaphore()
    for flipped in others:
        pl.semaphore_signal(barrier, inc=1, device_id=cube.beyond(place, flipped), device_id_type=MESH)
    pl.semaphore_wait(barrier, len(others))


def timetable(pieces, bits, offsets):
    steps = []
    for number, piece in enumerate(pieces):
        for stage in range(bits + 1):
            steps.append((piece[0] + offsets[stage], -piece[0], number, stage))
    return [(number, stage) for _, _, number, stage in sorted(steps)]


AXES = ("dp", "fsdp")


def pack_vectors(temporal, scales):
    upper = jnp.concatenate([temporal.T, jnp.pad(scales.T, ((0, 6), (0, 0)))], axis=1)
    return jnp.pad(upper, ((0, 0), (0, 128 - upper.shape[1])))


def divides(rows):
    return all(count % 16 == 0 for count in rows)


def scatter_plain(grads):
    sums = [lax.psum_scatter(g.astype(jnp.float32), AXES, scatter_dimension=0, tiled=True) for g in grads]
    squares = lax.psum(sum(jnp.sum(s * s) for s in sums), AXES)
    return sums, jnp.pad(squares[None, None], ((0, 7), (0, 127)))


def adam_kernel(count, norm_tile, *refs):
    grads, refs = refs[: count - 1], refs[count - 1 :]
    olds, ones, twos = (refs[i * count : (i + 1) * count] for i in range(3))
    norm_ref, refs = refs[3 * count], refs[3 * count + 1 :]
    rows_s, rows_t = olds[count - 2].shape[1], olds[count - 1].shape[1]
    views = [g[...] for g in grads[:-1]]
    views += [grads[-1][:2, rows_t : rows_t + rows_s], grads[-1][:, :rows_t]]
    afters, new_ones, new_twos = (
        refs[i * count : (i + 1) * count] for i in range(3)
    )
    grad_norm = jnp.sqrt(jnp.sum(norm_tile[...], keepdims=True))
    norm_ref[...] = grad_norm
    factor = CLIP_NORM / jnp.maximum(grad_norm, CLIP_NORM)
    for i in range(count):
        matrix = i < count - 2
        after, one, two = adam_update(
            olds[i][...],
            ones[i][...],
            twos[i][...],
            views[i],
            factor,
            RATE_MATRIX if matrix else RATE_VECTOR,
            WEIGHT_DECAY if matrix else 0.0,
        )
        afters[i][...] = after
        new_ones[i][...] = one
        new_twos[i][...] = two


def adam_all(norm_tile, grads, olds, ones, twos):
    count = len(olds)
    like = [jax.ShapeDtypeStruct(v.shape, v.dtype) for v in olds]
    return pl.pallas_call(
        functools.partial(adam_kernel, count),
        out_shape=[jax.ShapeDtypeStruct((1, 1), jnp.float32)] + like * 3,
        compiler_params=pltpu.CompilerParams(vmem_limit_bytes=VMEM_BYTES),
    )(norm_tile, *grads, *olds, *ones, *twos)


GELU_ONE = 0.7978845608028654
GELU_THREE = GELU_ONE * 0.044715
LANES = 128
ROWS = 8


def sigmoid(v):
    return 0.5 * jnp.tanh(0.5 * v) + 0.5


def gelu_parts(v):
    square = v * v
    turned = jnp.tanh(v * (GELU_ONE + GELU_THREE * square))
    half = 0.5 * turned + 0.5
    slope = half + (0.5 * v) * (1.0 - turned * turned) * (GELU_ONE + (3.0 * GELU_THREE) * square)
    return half, slope


def gelu_half(v):
    return 0.5 * jnp.tanh(v * (GELU_ONE + GELU_THREE * (v * v))) + 0.5


def one_less_exp(v, exp_v):
    series = 1.0 + v * (1.0 / 7.0)
    for order in (6.0, 5.0, 4.0, 3.0, 2.0):
        series = 1.0 + v * (1.0 / order) * series
    return jnp.where(v > -0.35, -v * series, 1.0 - exp_v)


def row_mask(width, first, last):
    rows = lax.broadcasted_iota(jnp.int32, (ROWS, width), 0)
    return (rows >= first) & (rows < last)


def shifted_down(now, before, steps, mask):
    return jnp.where(mask, pltpu.roll(now, steps, 0), pltpu.roll(before, steps, 0))


def shifted_up(now, after, steps, mask):
    return jnp.where(mask, pltpu.roll(now, ROWS - steps, 0), pltpu.roll(after, ROWS - steps, 0))


def wide(column, width):
    return column if width == LANES else jnp.concatenate([column] * (width // LANES), axis=1)


def rms_rows(source, gain, target, places):
    def one(tile, carry):
        rows = pl.ds(pl.multiple_of(tile * 16, 16), 16)
        v = source[rows, :].astype(jnp.float32)
        scale = lax.rsqrt(jnp.mean(v * v, axis=-1, keepdims=True) + NORM_EPSILON)
        target[rows, :] = (v * scale * gain[...]).astype(target.dtype)
        return carry

    lax.fori_loop(0, places // 16, one, 0, unroll=2)


def conv_forward(u, vec, masks, conv, lanes, width, places):
    taps = [jnp.broadcast_to(vec[k : k + 1, lanes], (ROWS, width)) for k in range(5)]
    inside = [row_mask(width, k, ROWS) for k in range(4)]

    def one(tile, before):
        parts = []
        for half in range(2):
            rows = pl.ds(pl.multiple_of(tile * 16 + half * 8, 8), ROWS)
            now = u[rows, lanes]
            total = taps[4] + now * taps[0]
            for k in range(1, 4):
                keep = wide(masks[k - 1, rows, :], width)
                total = total + shifted_down(now, before, k, inside[k]) * taps[k] * keep
            parts.append(total)
            before = now
        rows = pl.ds(pl.multiple_of(tile * 16, 16), 16)
        conv[rows, lanes] = jnp.concatenate(parts, axis=0).astype(conv.dtype)
        return before

    lax.fori_loop(0, places // 16, one, jnp.zeros((ROWS, width), jnp.float32), unroll=2)


def scan_tile(decay, value, masks, sign):
    for steps, mask in zip((1, 2, 4), masks):
        turn = steps if sign > 0 else ROWS - steps
        value = value + decay * jnp.where(mask, pltpu.roll(value, turn, 0), 0.0)
        decay = decay * jnp.where(mask, pltpu.roll(decay, turn, 0), 1.0)
    return decay, value


def mix_forward(recur, inlet, branch, conv, vec, masks, state, mixed, lanes, width, places):
    bias_r = jnp.broadcast_to(vec[5:6, lanes], (ROWS, width))
    bias_i = jnp.broadcast_to(vec[6:7, lanes], (ROWS, width))
    power = jnp.broadcast_to(vec[8:9, lanes], (ROWS, width))
    inside = [row_mask(width, k, ROWS) for k in (1, 2, 4)]

    def one(tile, carry):
        low_rows = pl.ds(pl.multiple_of(tile * 16, 16), 16)
        convs = conv[low_rows, lanes].astype(jnp.float32)
        parts = []
        for half in range(2):
            rows = pl.ds(pl.multiple_of(tile * 16 + half * 8, 8), ROWS)
            going = wide(masks[0, rows, :], width)
            gate_r = sigmoid(recur[rows, lanes] + bias_r)
            gate_i = sigmoid(inlet[rows, lanes] + bias_i)
            recur[rows, lanes] = gate_r
            inlet[rows, lanes] = gate_i
            log_decay = gate_r * power
            decay = jnp.exp(log_decay)
            scaling = jnp.sqrt(one_less_exp(2.0 * log_decay, decay * decay))
            scaling = scaling * going + (1.0 - going)
            value = scaling * gate_i * convs[half * 8 : half * 8 + 8]
            span, value = scan_tile(decay * going, value, inside, 1)
            value = value + span * carry
            carry = jnp.broadcast_to(value[ROWS - 1 : ROWS, :], (ROWS, width))
            state[rows, lanes] = value
            gate_b = branch[rows, lanes]
            parts.append(value * (gate_b * gelu_half(gate_b)))
        mixed[low_rows, lanes] = jnp.concatenate(parts, axis=0).astype(mixed.dtype)
        return carry

    lax.fori_loop(0, places // 16, one, jnp.zeros((ROWS, width), jnp.float32), unroll=2)


def mix_backward(
    grad, recur, inlet, branch, conv, state, vec, masks, low_r, low_i, direct, low_b, tallies, lanes, width, places
):
    power = jnp.broadcast_to(vec[8:9, lanes], (ROWS, width))
    below = [row_mask(width, 0, ROWS - k) for k in (1, 2, 4)]
    first = row_mask(width, 1, ROWS)
    tiles = places // 16
    nothing = jnp.zeros((ROWS, width), jnp.float32)

    def one(step, carries):
        carry, after, sum_r, sum_i, sum_p = carries
        tile = tiles - 1 - step
        low_rows = pl.ds(pl.multiple_of(tile * 16, 16), 16)
        convs = conv[low_rows, lanes].astype(jnp.float32)
        outs = [[None, None] for _ in range(4)]
        for half in (1, 0):
            at = tile * 16 + half * 8
            rows = pl.ds(pl.multiple_of(at, 8), ROWS)
            going = wide(masks[0, rows, :], width)
            gate_r, gate_i = recur[rows, lanes], inlet[rows, lanes]
            values = convs[half * 8 : half * 8 + 8]
            now = state[rows, lanes]
            earlier = state[pl.ds(pl.multiple_of(jnp.maximum(at - 8, 0), 8), ROWS), lanes]
            last = shifted_down(now, earlier, 1, first)
            log_decay = gate_r * power
            plain = jnp.exp(log_decay)
            square = plain * plain
            lost = one_less_exp(2.0 * log_decay, square)
            inverse = lax.rsqrt(lost)
            scaling = (lost * inverse) * going + (1.0 - going)
            gate_b = branch[rows, lanes]
            half_b, slope_b = gelu_parts(gate_b)
            mixed_grad = grad[rows, lanes]
            decay = plain * going
            later = shifted_up(decay, after, 1, below[0])
            span, total = scan_tile(later, mixed_grad * (gate_b * half_b), below, -1)
            total = total + span * carry
            carry = jnp.broadcast_to(total[0:1, :], (ROWS, width))
            after = decay
            outs[3][half] = mixed_grad * now * slope_b
            scaled = total * scaling
            flow = total * gate_i
            outs[2][half] = scaled * gate_i
            grad_i = scaled * values * (gate_i * (1.0 - gate_i))
            log_grad = going * (total * last * plain - flow * values * (square * inverse))
            grad_p = gate_r * log_grad
            grad_r = grad_p * ((1.0 - gate_r) * power)
            outs[0][half], outs[1][half] = grad_r, grad_i
            sum_r, sum_i, sum_p = sum_r + grad_r, sum_i + grad_i, sum_p + grad_p
        for target, parts in zip((low_r, low_i, direct, low_b), outs):
            target[low_rows, lanes] = jnp.concatenate(parts, axis=0).astype(target.dtype)
        return carry, after, sum_r, sum_i, sum_p

    sums = lax.fori_loop(0, tiles, one, (nothing,) * 5, unroll=2)[2:]
    tallies[5:6, lanes] = jnp.sum(sums[0], axis=0, keepdims=True)
    tallies[6:7, lanes] = jnp.sum(sums[1], axis=0, keepdims=True)
    tallies[7:8, lanes] = jnp.sum(sums[2], axis=0, keepdims=True) * vec[9:10, lanes]


def conv_backward(direct, u, vec, masks, low_u, tallies, lanes, width, places):
    taps = [jnp.broadcast_to(vec[k : k + 1, lanes], (ROWS, width)) for k in range(4)]
    inside = [row_mask(width, k, ROWS) for k in range(4)]
    below = [row_mask(width, 0, ROWS - k) for k in range(4)]
    tiles = places // 16
    nothing = jnp.zeros((ROWS, width), jnp.float32)

    def one(step, carries):
        afters, sums = list(carries[:3]), list(carries[3:])
        tile = tiles - 1 - step
        parts = [None, None]
        for half in (1, 0):
            at = tile * 16 + half * 8
            rows = pl.ds(pl.multiple_of(at, 8), ROWS)
            grad = direct[rows, lanes]
            now = u[rows, lanes]
            earlier = u[pl.ds(pl.multiple_of(jnp.maximum(at - 8, 0), 8), ROWS), lanes]
            total = grad * taps[0]
            sums[0] = sums[0] + grad * now
            sums[4] = sums[4] + grad
            for k in range(1, 4):
                kept = grad * wide(masks[k - 1, rows, :], width)
                total = total + taps[k] * shifted_up(kept, afters[k - 1], k, below[k])
                sums[k] = sums[k] + kept * shifted_down(now, earlier, k, inside[k])
                afters[k - 1] = kept
            parts[half] = total
        low_rows = pl.ds(pl.multiple_of(tile * 16, 16), 16)
        low_u[low_rows, lanes] = jnp.concatenate(parts, axis=0).astype(low_u.dtype)
        return (*afters, *sums)

    sums = lax.fori_loop(0, tiles, one, (nothing,) * 8, unroll=2)[3:]
    for k in range(5):
        tallies[k : k + 1, lanes] = jnp.sum(sums[k], axis=0, keepdims=True)


def product_into(target, lanes, first, second, pieces, extra=None):
    rows_in = first.shape[0] // pieces

    def one(piece, carry):
        rows = pl.ds(pl.multiple_of(piece * rows_in, rows_in), rows_in)
        total = jnp.dot(first[rows, :], second, preferred_element_type=jnp.float32)
        if extra is not None:
            total = total + extra[rows, lanes].astype(jnp.float32)
        target[rows, lanes] = total.astype(target.dtype)
        return carry

    lax.fori_loop(0, pieces, one, 0)


def mixer_forward_kernel(
    width, tokens, gain_one, gain_two, vec, masks, expand, gating, contract,
    normed, u, branch, recur, inlet, conv, state, mixed, middle, normed_two,
):
    places, channels = u.shape
    head = gating.shape[1] // 2
    rms_rows(tokens, gain_one, normed, places)

    def group(index, carry):
        lanes = pl.ds(pl.multiple_of(index * width, width), width)
        right = pl.ds(pl.multiple_of(channels + index * width, width), width)
        product_into(u, lanes, normed, expand[:, lanes], 2)
        product_into(branch, lanes, normed, expand[:, right], 2)
        conv_forward(u, vec, masks, conv, lanes, width, places)
        for part in range(width // head):
            spot = pl.ds(pl.multiple_of(index * width + part * head, head), head)
            logits = jnp.dot(conv[:, spot], gating[spot, :], preferred_element_type=jnp.float32)
            recur[:, spot] = logits[:, :head]
            inlet[:, spot] = logits[:, head:]
        mix_forward(recur, inlet, branch, conv, vec, masks, state, mixed, lanes, width, places)
        return carry

    lax.fori_loop(0, channels // width, group, 0)

    def column(index, carry):
        lanes = pl.ds(pl.multiple_of(index * 256, 256), 256)
        product_into(middle, lanes, mixed, contract[:, lanes], 2, tokens)
        return carry

    lax.fori_loop(0, middle.shape[1] // 256, column, 0)
    rms_rows(middle, gain_two, normed_two, places)


def mixer_forward(tokens, gain_one, gain_two, vec, masks, expand, gating, contract, width=256):
    places, features = tokens.shape
    channels = contract.shape[0]
    wide_f32 = jax.ShapeDtypeStruct((places, channels), jnp.float32)
    wide_low = jax.ShapeDtypeStruct((places, channels), BRAIN)
    return pl.pallas_call(
        functools.partial(mixer_forward_kernel, width),
        out_shape=[
            jax.ShapeDtypeStruct((places, features), BRAIN),
            wide_f32, wide_f32, wide_f32, wide_f32, wide_low, wide_f32, wide_low,
            jax.ShapeDtypeStruct((places, features), jnp.float32),
            jax.ShapeDtypeStruct((places, features), BRAIN),
        ],
        compiler_params=pltpu.CompilerParams(vmem_limit_bytes=VMEM_BYTES),
    )(tokens, gain_one, gain_two, vec, masks, expand, gating, contract)


def mixer_backward_kernel(
    width, low, contract, gating, vec, masks, u, branch, recur, inlet, conv, state,
    low_p, gating_grad, tallies, grad, direct, low_r, low_i,
):
    places, channels = u.shape
    head = gating.shape[1] // 2

    def group(index, carry):
        lanes = pl.ds(pl.multiple_of(index * width, width), width)
        right = pl.ds(pl.multiple_of(channels + index * width, width), width)
        total = lax.dot_general(
            low[...], contract[lanes, :], (((1,), (1,)), ((), ())), preferred_element_type=jnp.float32
        )
        grad[...] = total
        here = slice(0, width)
        views = [v.at[:, lanes] for v in (recur, inlet, branch, conv, state)]
        mix_backward(
            grad, *views, vec.at[:, lanes], masks, low_r, low_i, direct,
            low_p.at[:, right], tallies.at[:, lanes], here, width, places,
        )
        for part in range(width // head):
            spot = slice(part * head, (part + 1) * head)
            at = pl.ds(pl.multiple_of(index * width + part * head, head), head)
            low_both = jnp.concatenate([low_r[:, spot], low_i[:, spot]], axis=1)
            gating_grad[at, :] = lax.dot_general(
                conv[:, at], low_both, (((0,), (0,)), ((), ())), preferred_element_type=jnp.float32
            ).astype(gating_grad.dtype)
            direct[:, spot] += lax.dot_general(
                low_both, gating[at, :], (((1,), (1,)), ((), ())), preferred_element_type=jnp.float32
            )
        conv_backward(
            direct, u.at[:, lanes], vec.at[:, lanes], masks, low_p.at[:, lanes], tallies.at[:, lanes],
            here, width, places,
        )
        return carry

    lax.fori_loop(0, channels // width, group, 0)


def mixer_backward(low, contract, gating, vec, masks, u, branch, recur, inlet, conv, state, width=256):
    places, channels = u.shape
    return pl.pallas_call(
        functools.partial(mixer_backward_kernel, width),
        out_shape=[
            jax.ShapeDtypeStruct((places, 2 * channels), BRAIN),
            jax.ShapeDtypeStruct(gating.shape, BRAIN),
            jax.ShapeDtypeStruct((8, channels), jnp.float32),
        ],
        scratch_shapes=[
            pltpu.VMEM((places, width), jnp.float32),
            pltpu.VMEM((places, width), jnp.float32),
            pltpu.VMEM((places, width), BRAIN),
            pltpu.VMEM((places, width), BRAIN),
        ],
        compiler_params=pltpu.CompilerParams(vmem_limit_bytes=VMEM_BYTES),
    )(low, contract, gating, vec, masks, u, branch, recur, inlet, conv, state)


def channel_rows(temporal_rows):
    decay = temporal_rows[7:8]
    power = -GATE_POWER * jax.nn.softplus(-decay)
    slope = GATE_POWER * jax.nn.sigmoid(-decay)
    return jnp.concatenate([temporal_rows, power, slope, jnp.zeros_like(temporal_rows)[:6]], axis=0)


def keep_masks(lengths, length):
    starts = jnp.cumsum(lengths) - lengths
    places = jnp.arange(length, dtype=jnp.int32)
    resets = jnp.any(places[:, None] == starts[None, :], axis=-1)
    one = 1.0 - resets.astype(jnp.float32)
    two = one * jnp.concatenate([jnp.zeros((1,)), one[:-1]])
    three = two * jnp.concatenate([jnp.zeros((2,)), one[:-2]])
    return jnp.broadcast_to(jnp.stack([one, two, three])[:, :, None], (3, length, LANES))


def rms_pull(values, gain, grad):
    scale = lax.rsqrt(jnp.mean(values * values, axis=-1, keepdims=True) + NORM_EPSILON)
    scaled = grad * gain
    inner = jnp.mean(values * scaled, axis=-1, keepdims=True)
    return scale * scaled - values * (scale * scale * scale * inner), jnp.sum(grad * values * scale, axis=0)


def gather_plan():
    pairs = [(0, 1), (0, 1), (2, 3)] * 10
    expand = [(i, pairs[i][j], 12 * j + 2 * i, 2) for i in range(6) for j in range(2)]
    contract = [(6, 2, 0, 2), (6, 3, 2, 2), (7, 0, 4, 2), (7, 1, 6, 2)]
    widen = [(12 + i, pairs[i][j], 24 * j + 2 * i, 2) for i in range(12) for j in range(2)]
    narrow = [(8 + i, pairs[i][j], 2 * i + j, 1) for i in range(4) for j in range(2)]
    return [(0, 0, 0, 1)], expand, [(6, 0, 0, 1), (6, 1, 1, 1)], contract, widen, narrow


SLOT_US = 6.2
AG_OFF = (0, 2, 4, 6, 8, 10)


def plan_pieces(cube, plan):
    orders = cube.orders()
    pieces = []
    for array, cuts in enumerate(plan):
        for group, order, first, tiles in cuts:
            pieces.append((group, array, first * 128, tiles * 128, orders[order]))
    return sorted(pieces, key=lambda piece: piece[0])


def interleave(events, works):
    now = 0.0
    at = 0
    for length, needed, call in works:
        while at < needed or (at < len(events) and events[at][0] <= now):
            now = max(now, events[at][0])
            events[at][1]()
            at += 1
        call()
        now += length
    for _, call in events[at:]:
        call()


def fill_vectors(cube, misc, vec, gains, rows_t, rows_s):
    lane = lax.broadcasted_iota(jnp.int32, (8, LANES), 1)

    def spread(target, first, count):
        tiles = [jnp.zeros((8, LANES), jnp.float32) for _ in range(target.shape[1] // LANES)]
        for device in range(1 << cube.bits):
            spot = tuple((device >> (cube.bits - 1 - i)) % 2 for i in range(cube.bits))
            tile, start = divmod(device * count, LANES)
            turned = pltpu.roll(misc[spot], (start - first) % LANES, 1)
            tiles[tile] = jnp.where((lane >= start) & (lane < start + count), turned, tiles[tile])
            if start + count > LANES:
                tiles[tile + 1] = jnp.where(lane < start + count - LANES, turned, tiles[tile + 1])
        for i, tile in enumerate(tiles):
            target[0:8, i * LANES : (i + 1) * LANES] = tile

    spread(vec, 0, rows_t)
    spread(gains, rows_t, rows_s)
    decay = vec[7:8, :]
    small = jnp.exp(-jnp.abs(decay))
    vec[8:9, :] = -GATE_POWER * (jnp.maximum(-decay, 0.0) + jnp.log(1.0 + small))
    vec[9:10, :] = GATE_POWER * sigmoid(-decay)


def fill_masks(lengths, masks, places):
    starts = [jnp.int32(0)]
    for document in range(lengths.shape[1] - 1):
        starts.append(starts[-1] + lengths[0, document])

    def one(tile, carry):
        rows = pl.ds(pl.multiple_of(tile * 8, 8), 8)
        place = tile * 8 + lax.broadcasted_iota(jnp.int32, (8, LANES), 0)
        keep = jnp.ones((8, LANES), jnp.float32)
        for k in range(3):
            for start in starts:
                keep = jnp.where(place == start + k, 0.0, keep)
            masks[k, rows, :] = keep
        return carry

    lax.fori_loop(0, places // 8, one, 0)


def turn_into(target, source, first):
    columns = source.shape[1]

    def one(piece, carry):
        rows = pl.ds(pl.multiple_of(piece * 128, 128), 128)
        target[first : first + columns, rows] = source[rows, :].T
        return carry

    lax.fori_loop(0, source.shape[0] // 128, one, 0)


def forward_kernel(cube, pieces, width, vector_rows, *refs):
    (lengths, tokens, upstream, misc, *shards_in) = refs[:9]
    (expand_out, gating_out, contract_out, widen_out, narrow_out) = refs[9:14]
    head_outs = refs[14:20]
    (normed_t_out, mixed_t_out, pulled_out, active_t_out, block_out) = refs[20:25]
    (middle, normed_two_t, vec, gains, masks) = refs[25:30]
    (misc_full, expand_full, gating_full, contract_full, widen_full) = refs[30:35]
    heads = refs[35:41]
    (u, branch, recur, inlet, state, conv) = heads
    (mixed, normed, normed_two, normed_t, mixed_t, gates_in, ups, pulls, pulled) = refs[41:50]
    (active, active_t, narrow_tile, block_low) = refs[50:54]
    held = refs[54:59]
    (own_sem, send_sem, recv_sem, full_sem, head_sem, turn_sem, feed_sem, widen_sem, tile_sem) = refs[59:]
    places, channels = u.shape
    hidden, features = active_t_out.shape[0], tokens.shape[1]
    head = gating_full.shape[-1] // 2
    groups, tiles = channels // width, hidden // width
    bits = cube.bits
    whole = (slice(None),) * bits
    fulls = (misc_full, expand_full, gating_full, contract_full, widen_full, narrow_out)
    place = cube.place()
    greet(cube, place)
    own = [pltpu.make_async_copy(misc, fulls[0].at[tuple(place)], own_sem.at[0])]
    own[0].start()
    for i, (source, low) in enumerate(zip(shards_in, held)):
        low[...] = source[...].astype(BRAIN)
        own.append(pltpu.make_async_copy(low, fulls[i + 1].at[tuple(place)], own_sem.at[i + 1]))
        own[-1].start()

    def exchange(number, stage):
        _, array, first, columns, order = pieces[number]
        spot = tuple(slice(None) if bit in order[:stage] else place[bit] for bit in range(bits))
        window = slice(None) if array == 0 else pl.ds(first, columns)
        view = fulls[array].at[spot + (slice(None), window)]
        return pltpu.make_async_remote_copy(
            src_ref=view,
            dst_ref=view,
            send_sem=send_sem.at[number, stage],
            recv_sem=recv_sem.at[number, stage],
            device_id=cube.partner(place, order[stage]),
            device_id_type=MESH,
        )

    waited = set()

    def event(number, stage):
        array = pieces[number][1]
        if stage == 0 and array not in waited:
            waited.add(array)
            own[array].wait()
        if stage > 0:
            exchange(number, stage - 1).wait_recv()
        if stage < bits:
            exchange(number, stage).start()

    steps = timetable(pieces, bits, AG_OFF)
    events = [
        ((pieces[number][0] + AG_OFF[stage]) * SLOT_US, functools.partial(event, number, stage))
        for number, stage in steps
    ]
    arrived = {}
    for i, (number, stage) in enumerate(steps):
        if stage == bits:
            arrived[pieces[number][0]] = i + 1

    kept = []

    def keep(source, target, sem):
        copy = pltpu.make_async_copy(source, target, sem)
        copy.start()
        kept.append(copy)

    def weight(full, first, columns):
        return full[whole + (slice(None), slice(first, first + columns))].reshape(-1, columns)

    def begin():
        fill_masks(lengths, masks, places)

    def vectors():
        fill_vectors(cube, misc_full, vec, gains, *vector_rows)
        rms_rows(tokens, gains.at[0:1, :], normed, places)

    def turn():
        turn_into(normed_t, normed, 0)
        keep(normed_t, normed_t_out, turn_sem.at[0])

    def project(group):
        lanes = slice(group * width, group * width + width)
        product_into(u, lanes, normed, weight(expand_full, group * width, width), 1)
        product_into(branch, lanes, normed, weight(expand_full, channels + group * width, width), 1)
        conv_forward(u, vec, masks, conv, lanes, width, places)

    def gates(group):
        gating = gating_full[whole].reshape(-1, 2 * head)
        for part in range(width // head):
            spot = slice(group * width + part * head, group * width + (part + 1) * head)
            logits = jnp.dot(conv[:, spot], gating[spot], preferred_element_type=jnp.float32)
            recur[:, spot] = logits[:, :head]
            inlet[:, spot] = logits[:, head:]

    def mix(group):
        lanes = slice(group * width, group * width + width)
        mix_forward(recur, inlet, branch, conv, vec, masks, state, mixed, lanes, width, places)
        for index in range(len(heads)):
            keep(heads[index].at[:, lanes], head_outs[index].at[:, lanes], head_sem.at[index, group])
        turn_into(mixed_t, mixed.at[:, lanes], group * width)

    def join(index):
        lanes = slice(index * 256, index * 256 + 256)
        product_into(middle, lanes, mixed, weight(contract_full, index * 256, 256), 1, tokens)

    def finish():
        rms_rows(middle, gains.at[1:2, :], normed_two, places)
        turn_into(normed_two_t, normed_two, 0)
        keep(mixed_t, mixed_t_out, turn_sem.at[1])
        keep(expand_full, expand_out, full_sem.at[0])
        keep(gating_full, gating_out, full_sem.at[1])
        keep(contract_full, contract_out, full_sem.at[2])

    fed = {}
    tile_loads = {}
    narrow_rows = shards_in[4].shape[0]

    def load_tile(tile):
        copies, row = [], tile * width
        while row < (tile + 1) * width:
            device, first = divmod(row, narrow_rows)
            count = min(narrow_rows - first, (tile + 1) * width - row)
            spot = tuple((device >> (bits - 1 - i)) % 2 for i in range(bits))
            copies.append(
                pltpu.make_async_copy(
                    narrow_out.at[spot + (pl.ds(first, count), slice(None))],
                    narrow_tile.at[tile % 2, pl.ds(row - tile * width, count), :],
                    tile_sem.at[tile % 2, len(copies)],
                )
            )
            copies[-1].start()
            row += count
        return copies

    def feed(tile):
        slot = tile % 2
        lanes = slice(tile * width, tile * width + width)
        if tile == 0:
            for copy in kept:
                copy.wait()
            kept.clear()
            tile_loads[0] = load_tile(0)
        if tile + 1 < tiles:
            tile_loads[tile + 1] = load_tile(tile + 1)
        for copy in fed.pop(tile - 2, ()):
            copy.wait()
        for part, first in enumerate((tile * width, hidden + tile * width)):
            window = whole + (slice(None), pl.ds(first, width))
            keep(widen_full.at[window], widen_out.at[window], widen_sem.at[part, tile])
        here = slice(0, width)
        product_into(gates_in, here, normed_two, weight(widen_full, tile * width, width), 1)
        product_into(ups, here, normed_two, weight(widen_full, hidden + tile * width, width), 1)
    def pull(tile):
        slot = tile % 2
        for copy in tile_loads.pop(tile):
            copy.wait()

        pulls[...] = lax.dot_general(
            upstream[...], narrow_tile[slot], (((1,), (1,)), ((), ())), preferred_element_type=jnp.float32
        )

        def one(step, carry):
            rows = pl.ds(pl.multiple_of(step * 16, 16), 16)
            gate, up, back = gates_in[rows, :], ups[rows, :], pulls[rows, :]
            half, slope = gelu_parts(gate)
            curved = gate * half
            pulled[slot, rows, 0:width] = (back * (up * slope)).astype(BRAIN)
            pulled[slot, rows, width : 2 * width] = (back * curved).astype(BRAIN)
            active[rows, :] = (curved * up).astype(BRAIN)
            return carry

        lax.fori_loop(0, places // 16, one, 0, unroll=2)

    def spread(tile):
        slot = tile % 2
        lanes = slice(tile * width, tile * width + width)
        for first in range(0, features, 512):
            columns = slice(first, first + 512)
            total = jnp.dot(active[...], narrow_tile[slot, :, columns], preferred_element_type=jnp.float32)
            total = total + (middle[:, columns] if tile == 0 else u[:, columns])
            if tile == tiles - 1:
                block_low[:, columns] = total.astype(BRAIN)
            else:
                u[:, columns] = total
        turn_into(active_t.at[slot], active, 0)
        copies = [
            pltpu.make_async_copy(pulled.at[slot], pulled_out.at[tile], feed_sem.at[0, slot]),
            pltpu.make_async_copy(active_t.at[slot], active_t_out.at[lanes, :], feed_sem.at[1, slot]),
        ]
        if tile == tiles - 1:
            copies.append(pltpu.make_async_copy(block_low, block_out, turn_sem.at[2]))
        for copy in copies:
            copy.start()
        fed[tile] = copies

    works = [(1.0, 0, begin), (3.0, arrived[0], vectors), (1.0, 0, turn)]
    for group in range(groups):
        works.append((2.5, arrived[group], functools.partial(project, group)))
    for group in range(groups):
        works.append((0.3, arrived[6], functools.partial(gates, group)))
        works.append((3.5, 0, functools.partial(mix, group)))
    for index in range(middle.shape[1] // 256):
        works.append((0.8, arrived[7], functools.partial(join, index)))
    works.append((2.0, 0, finish))
    for tile in range(tiles):
        works.append((1.6, max(arrived[12 + tile], arrived[11]), functools.partial(feed, tile)))
        works.append((1.6, 0, functools.partial(pull, tile)))
        works.append((1.3, 0, functools.partial(spread, tile)))
    interleave(events, works)
    for copies in fed.values():
        for copy in copies:
            copy.wait()
    for copy in kept:
        copy.wait()
    for number in range(len(pieces)):
        for stage in range(bits):
            exchange(number, stage).wait_send()


def forward_all(cube, lengths, tokens, upstream, misc, matrices, vector_rows, width=256):
    places, features = tokens.shape
    channels, hidden = matrices[2].shape[0] << cube.bits, matrices[4].shape[0] << cube.bits
    pieces = plan_pieces(cube, gather_plan())
    pair = (2,) * cube.bits
    tiles = hidden // width
    heads = [((places, channels), jnp.float32)] * 5 + [((places, channels), BRAIN)]
    full = [(pair + m.shape, BRAIN) for m in matrices]
    turned = [((features, places), BRAIN), ((channels, places), BRAIN)]
    row = ((places, features), BRAIN)
    hbm = full + heads + turned
    hbm += [((tiles, places, 2 * width), BRAIN), ((hidden, places), BRAIN), row]
    vmem = [
        ((places, features), jnp.float32),
        ((features, places), BRAIN),
        ((16, channels), jnp.float32),
        ((8, features), jnp.float32),
        ((3, places, LANES), jnp.float32),
    ]
    scratch = [(pair + misc.shape, jnp.float32)] + full[:4] + heads + [((places, channels), BRAIN)]
    scratch += [row] * 2 + turned + [((places, width), jnp.float32)] * 3
    scratch += [((2, places, 2 * width), BRAIN), ((places, width), BRAIN), ((2, width, places), BRAIN)]
    scratch += [((2, width, features), BRAIN), row]
    scratch += [(m.shape, BRAIN) for m in matrices]
    stages = (len(pieces), cube.bits)
    most = width // matrices[4].shape[0] + 2
    sems = [(6,), stages, stages, (3,), (len(heads), channels // width), (3,), (2, 2), (2, tiles), (2, most)]
    outs = pl.pallas_call(
        functools.partial(forward_kernel, cube, pieces, width, vector_rows),
        out_shape=[jax.ShapeDtypeStruct(*like) for like in hbm + vmem],
        in_specs=[pl.BlockSpec(memory_space=pltpu.SMEM)] + [pl.BlockSpec(memory_space=pltpu.VMEM)] * 8,
        out_specs=[pl.BlockSpec(memory_space=pl.ANY)] * len(hbm)
        + [pl.BlockSpec(memory_space=pltpu.VMEM)] * len(vmem),
        scratch_shapes=[pltpu.VMEM(*like) for like in scratch]
        + [pltpu.SemaphoreType.DMA(shape) for shape in sems],
        compiler_params=pltpu.CompilerParams(
            collective_id=2, has_side_effects=True, vmem_limit_bytes=FORWARD_BYTES
        ),
    )(lengths, tokens, upstream, misc, *matrices)
    return [g.reshape((-1,) + g.shape[cube.bits + 1 :]) for g in outs[:5]], outs[5:]


FORWARD_BYTES = 63 * 1024 * 1024


class Pump:
    def __init__(self):
        self.now, self.link, self.queue, self.done = 0.0, 0.0, [], set()

    def later(self, time, key, call):
        self.queue.append((time, len(self.queue), key, call))

    def step(self):
        first = min(self.queue, key=lambda entry: entry[:2])
        self.queue = [(e if e is not first else None) for e in self.queue]
        self.queue = [e for e in self.queue if e is not None]
        self.now = max(self.now, first[0])
        self.done.add(first[2])
        first[3]()

    def run(self, length, needed, call):
        while self.queue and (
            min(entry[0] for entry in self.queue) <= self.now or not self.done.issuperset(needed)
        ):
            self.step()
        self.now += length
        call()

    def finish(self):
        while self.queue:
            self.step()


class Piece:
    def __init__(self, number, array, first, columns, order, source, source_first):
        self.number, self.array, self.first, self.columns = number, array, first, columns
        self.order, self.source, self.source_first = order, source, source_first


CORE_US = 2.0
LAG_US = 12.0
RATE_US = 95.0 / 29.1e6


def pull_rows(values, grad, gain, emit, places):
    def one(tile, total):
        rows = pl.ds(pl.multiple_of(tile * 16, 16), 16)
        v, g = values(rows), grad[rows, :]
        scale = lax.rsqrt(jnp.mean(v * v, axis=-1, keepdims=True) + NORM_EPSILON)
        scaled = g * gain[...]
        inner = jnp.mean(v * scaled, axis=-1, keepdims=True)
        emit(rows, scale * scaled - v * (scale * scale * scale * inner))
        term = g * v * scale
        return total + term[0:8] + term[8:16]

    return lax.fori_loop(0, places // 16, one, jnp.zeros((8, grad.shape[1]), jnp.float32))


def pack_tiles(cube, tallies, scale_grads, staging):
    lane = lax.broadcasted_iota(jnp.int32, (8, LANES), 1)
    devices = 1 << cube.bits
    count_t, count_s = tallies.shape[1] // devices, scale_grads.shape[1] // devices

    def cut(source, device, count, at):
        tile, start = divmod(device * count, LANES)
        got = pltpu.roll(source[:, tile * LANES : (tile + 1) * LANES], (at - start) % LANES, 1)
        if start + count > LANES:
            more = pltpu.roll(source[:, (tile + 1) * LANES : (tile + 2) * LANES], (at - start) % LANES, 1)
            got = jnp.where(lane < at + LANES - start, got, more)
        return got

    for device in range(devices):
        spot = tuple((device >> (cube.bits - 1 - i)) % 2 for i in range(cube.bits))
        first = cut(tallies, device, count_t, 0)
        second = cut(scale_grads, device, count_s, count_t)
        tile = jnp.where(lane < count_t, first, jnp.where(lane < count_t + count_s, second, 0.0))
        staging[spot] = tile


def backward_kernel(cube, width, *refs):
    (cot_in, normed_two_t_in, active_t_in, pulled, widen, contract, expand) = refs[:7]
    (middle, normed_t_in, mixed_t_in, tokens_in, u, branch, recur, inlet, state, conv) = refs[7:17]
    (gating, vec, gains, masks) = refs[17:21]
    tokens_grad_out, sums, norm = refs[21], refs[22:28], refs[28]
    refs = refs[29:]
    bits = cube.bits
    inbox = [refs[6 * stage : 6 * stage + 6] for stage in range(bits)]
    refs = refs[6 * bits :]
    (stage_s, stage_n, stage_c, stage_g, stage_m, flat_g, cot, normed_two_t, tall, acc, middle_grad) = refs[:11]
    (middle_low, wide_f, wide_w, wide_n, wide_c, pairs, low_r, low_i, grad, direct) = refs[11:21]
    (tallies, scale_grads, partial, other) = refs[21:25]
    (send_sem, recv_sem, load_sem, f_sem, w_sem, n_sem, c_sem, norm_send, norm_recv, out_sem, pair_sem) = refs[25:]
    places, features = cot.shape
    channels, hidden = conv.shape[1], tall.shape[0]
    head = gating.shape[1] // 2
    tiles, groups = hidden // width, channels // width
    devices = 1 << bits
    place = cube.place()
    orders = cube.orders()
    pump = Pump()
    pieces = []

    def load(source, target, sem):
        copy = pltpu.make_async_copy(source, target, sem)
        copy.start()
        return copy

    load_cot = load(cot_in, cot, load_sem.at[0])
    load_active = load(active_t_in, tall, load_sem.at[1])
    load_two = load(normed_two_t_in, normed_two_t, load_sem.at[2])
    spare = wide_f.shape[0] - features // width
    load_middle = [
        load(middle.at[:, pl.ds(i * width, width)], wide_f.at[spare + i], f_sem.at[spare + i])
        for i in range(features // width)
    ]

    def load_feed(tile):
        slot, lanes = tile % 2, pl.ds(tile * width, width)
        right = pl.ds(hidden + tile * width, width)
        return (
            load(pulled.at[tile], pairs.at[slot], pair_sem.at[slot]),
            load(widen.at[:, lanes], wide_w.at[slot, :, pl.ds(0, width)], w_sem.at[slot, 0]),
            load(widen.at[:, right], wide_w.at[slot, :, pl.ds(width, width)], w_sem.at[slot, 1]),
        )

    heads = (recur, inlet, branch, state, u)

    def load_head(group):
        slot, lanes = group % 2, pl.ds(group * width, width)
        right = pl.ds(channels + group * width, width)
        copies = [
            load(source.at[:, lanes], wide_f.at[5 * slot + i], f_sem.at[5 * slot + i])
            for i, source in enumerate(heads)
        ]
        return copies + [
            load(conv.at[:, lanes], wide_c.at[slot], c_sem.at[slot]),
            load(contract.at[lanes, :], wide_n.at[slot], n_sem.at[slot]),
            load(expand.at[:, lanes], wide_w.at[slot, :, pl.ds(0, width)], w_sem.at[slot, 0]),
            load(expand.at[:, right], wide_w.at[slot, :, pl.ds(width, width)], w_sem.at[slot, 1]),
        ]

    greet(cube, place, [flipped for members in cube.circles() for flipped in cube.subsets(members)])
    partial[0] = jnp.zeros(partial.shape[1:], jnp.float32)
    loads = {0: load_feed(0)}

    def left_at(piece, stage):
        return [bit for bit in range(bits) if bit not in piece.order[bits - stage :]]

    def exchange(piece, stage):
        bit = piece.order[bits - 1 - stage]
        left = left_at(piece, stage)
        source = piece.source if stage == 0 else inbox[stage - 1][piece.array]
        first = piece.source_first if stage == 0 else piece.first
        spot = tuple(1 - place[bit] if b == bit else slice(None) for b in left)
        rest = (slice(None),) * (len(left) - 1)
        return pltpu.make_async_remote_copy(
            src_ref=source.at[spot + (slice(None), pl.ds(first, piece.columns))],
            dst_ref=inbox[stage][piece.array].at[rest + (slice(None), pl.ds(piece.first, piece.columns))],
            send_sem=send_sem.at[piece.number, stage],
            recv_sem=recv_sem.at[piece.number, stage],
            device_id=cube.partner(place, bit),
            device_id_type=MESH,
        )

    def add(piece, stage):
        bit = piece.order[bits - 1 - stage]
        left = left_at(piece, stage)
        after = [b for b in left if b != bit]
        source = piece.source if stage == 0 else inbox[stage - 1][piece.array]
        first = piece.source_first if stage == 0 else piece.first
        target = inbox[stage][piece.array]
        window = (slice(None), slice(piece.first, piece.first + piece.columns))
        source_window = (slice(None), slice(first, first + piece.columns))

        inner = min(len(after), 2)

        def one(step, carry):
            outer = [lax.rem(step // (1 << (len(after) - inner - 1 - i)), 2) for i in range(len(after) - inner)]
            for block in range(1 << inner):
                spot = tuple(outer + [(block >> (inner - 1 - i)) % 2 for i in range(inner)])
                mine_at = list(spot)
                mine_at.insert(left.index(bit), place[bit])
                mine, theirs = source[tuple(mine_at) + source_window], target[spot + window]
                if stage < bits - 1:
                    target[spot + window] = mine + theirs
                    continue
                total = mine.astype(jnp.float32) + theirs.astype(jnp.float32)
                sums[piece.array][window] = total
                squares = total * total
                tile = squares.reshape(squares.shape[0] // 8, 8, piece.columns).sum(axis=0)
                for start in range(0, piece.columns, LANES):
                    partial[0] += tile[:, start : start + LANES]
            return carry

        lax.fori_loop(0, 1 << (len(after) - inner), one, 0)

    def settle(piece):
        exchange(piece, 0).wait_recv()
        exchange(piece, 0).wait_send()
        add(piece, 0)

    def event(piece, stage):
        exchange(piece, stage - 1).wait_recv()
        add(piece, stage - 1)
        if stage < bits:
            exchange(piece, stage).start()

    def begin(array, first, columns, order, source, source_first):
        piece = Piece(len(pieces), array, first, columns, orders[order], source, source_first)
        pieces.append(piece)
        exchange(piece, 0).start()
        start = max(pump.now + CORE_US, pump.link)
        length = devices * inbox[0][array].shape[-2] * columns * 2 * RATE_US
        pump.link = start + length
        pump.later(pump.now + CORE_US, (piece.number, 0), functools.partial(settle, piece))
        pump.later(start, (piece.number, 1), lambda: exchange(piece, 1).start())
        for stage in range(2, bits + 1):
            time = start + length + LAG_US * (stage - 1)
            pump.later(time, (piece.number, stage), functools.partial(event, piece, stage))
        return (piece.number, 0)

    turns = [0]

    def next_orders():
        turns[0] += 1
        return (2, 3) if turns[0] % 3 == 0 else (0, 1)

    freed = {}

    def product_stage(target, first, second):
        parts = 1 << bit_count(first.shape[0] // PRODUCT_ROWS)
        rows_in = first.shape[0] // parts
        fixed = bit_count(parts)
        shape = (2,) * (bits - fixed) + target.shape[bits:-1] + (256,)
        for start in range(0, second.shape[1], 256):
            columns = slice(start, start + 256)
            rest = (slice(None),) * (bits - fixed + 1) + (columns,)

            def one(piece, carry):
                rows = pl.ds(pl.multiple_of(piece * rows_in, rows_in), rows_in)
                total = jnp.dot(first[rows, :], second[:, columns], preferred_element_type=jnp.float32)
                spot = tuple(lax.rem(piece // (1 << (fixed - 1 - i)), 2) for i in range(fixed))
                target[spot + rest] = total.astype(target.dtype).reshape(shape)
                return carry

            lax.fori_loop(0, parts, one, 0)

    def accumulate(target, first, second, fresh):
        def one(piece, carry):
            columns = pl.ds(pl.multiple_of(piece * 256, 256), 256)
            total = lax.dot_general(
                first[...], second[columns, :], (((1,), (1,)), ((), ())), preferred_element_type=jnp.float32
            )
            target[:, columns] = total if fresh else target[:, columns] + total
            return carry

        lax.fori_loop(0, target.shape[1] // 256, one, 0)

    def narrow_grads(index):
        if index == 0:
            load_cot.wait()
            load_active.wait()
        slot = index % 2
        product_stage(stage_n.at[slot], tall, cot.at[:, pl.ds(index * width, width)])
        freed[slot, 1] = [begin(5, index * width, width, index, stage_n.at[slot], 0)]

    def feed(tile):
        slot = tile % 2
        if tile + 1 < tiles:
            loads[tile + 1] = load_feed(tile + 1)
        if tile == 0:
            load_two.wait()
        for copy in loads.pop(tile):
            copy.wait()

        product_stage(stage_s.at[slot], normed_two_t, pairs.at[slot])
        first, second = next_orders()
        freed[slot, 0] = [
            begin(4, tile * width, width, first, stage_s.at[slot], 0),
            begin(4, hidden + tile * width, width, second, stage_s.at[slot], width),
        ]
        accumulate(acc, pairs.at[slot], wide_w.at[slot], tile == 0)

    def pull_middle():
        loads[0] = load_head(0)
        for copy in load_middle:
            copy.wait()

        def values(rows):
            return jnp.concatenate([wide_f[spare + i, rows, :] for i in range(features // width)], axis=1)

        def emit(rows, total):
            total = total + cot[rows, :].astype(jnp.float32)
            middle_grad[rows, :] = total
            middle_low[rows, :] = total.astype(BRAIN)

        total = pull_rows(values, acc, gains.at[1:2, :], emit, places)
        scale_grads[...] = jnp.zeros_like(scale_grads)
        scale_grads[1:2, :] = jnp.sum(total, axis=0, keepdims=True)

    def load_tall():
        return (
            load(normed_t_in, tall.at[pl.ds(0, features), :], load_sem.at[3]),
            load(mixed_t_in, tall.at[pl.ds(features, channels), :], load_sem.at[4]),
            load(tokens_in, cot, load_sem.at[5]),
        )

    def contract_grads(index):
        if index == 0:
            for copy in load_turned:
                copy.wait()
        slot = index % 2
        lanes = pl.ds(index * width, width)
        product_stage(stage_c.at[slot], tall.at[pl.ds(features, channels), :], middle_low.at[:, lanes])
        freed[slot, 2] = [begin(3, index * width, width, index, stage_c.at[slot], 0)]

    here = slice(0, width)

    def mix(group):
        slot = group % 2
        lanes = pl.ds(group * width, width)
        if group + 1 < groups:
            loads[group + 1] = load_head(group + 1)
        for copy in loads.pop(group):
            copy.wait()
        grad[...] = lax.dot_general(
            middle_low[...], wide_n[slot], (((1,), (1,)), ((), ())), preferred_element_type=jnp.float32
        )
        views = [wide_f.at[5 * slot + i] for i in range(5)]
        mix_backward(
            grad, views[0], views[1], views[2], wide_c.at[slot], views[3], vec.at[:, lanes], masks,
            low_r, low_i, direct, pairs.at[0, :, pl.ds(width, width)], tallies.at[:, lanes], here, width, places,
        )

    def unmix(group):
        slot = group % 2
        lanes = pl.ds(group * width, width)
        for part in range(width // head):
            spot = slice(part * head, (part + 1) * head)
            at = pl.ds(group * width + part * head, head)
            low_both = jnp.concatenate([low_r[:, spot], low_i[:, spot]], axis=1)
            flat_g[at, :] = lax.dot_general(
                wide_c[slot, :, spot], low_both, (((0,), (0,)), ((), ())), preferred_element_type=jnp.float32
            ).astype(BRAIN)
            direct[:, spot] += lax.dot_general(
                low_both, gating[at, :], (((1,), (1,)), ((), ())), preferred_element_type=jnp.float32
            )
        conv_backward(
            direct, wide_f.at[5 * slot + 4], vec.at[:, lanes], masks, pairs.at[0, :, pl.ds(0, width)],
            tallies.at[:, lanes], here, width, places,
        )

    def expand_grads(group):
        slot = group % 2
        product_stage(stage_s.at[slot], tall.at[pl.ds(0, features), :], pairs.at[0])
        first, second = next_orders()
        freed[slot, 0] = [
            begin(1, group * width, width, first, stage_s.at[slot], 0),
            begin(1, channels + group * width, width, second, stage_s.at[slot], width),
        ]
        accumulate(acc, pairs.at[0], wide_w.at[slot], group == 0)

    def gating_grads():
        rows_in = flat_g.shape[0] // devices

        def one(device, carry):
            spot = tuple(lax.rem(device // (1 << (bits - 1 - i)), 2) for i in range(bits))
            stage_g[spot] = flat_g[pl.ds(pl.multiple_of(device * rows_in, 16), rows_in), :]
            return carry

        lax.fori_loop(0, devices, one, 0)
        begin(2, 0, head, 0, stage_g, 0)
        begin(2, head, head, 1, stage_g, head)

    def finish():
        def values(rows):
            return cot[rows, :].astype(jnp.float32)

        def emit(rows, total):
            middle_low[rows, :] = (middle_grad[rows, :] + total).astype(BRAIN)

        total = pull_rows(values, acc, gains.at[0:1, :], emit, places)
        load(middle_low, tokens_grad_out, out_sem.at[0])
        scale_grads[0:1, :] = jnp.sum(total, axis=0, keepdims=True)
        pack_tiles(cube, tallies, scale_grads, stage_m)
        begin(0, 0, LANES, 0, stage_m, 0)

    def run(length, call, *keys):
        needed = [key for slot in keys for key in freed.get(slot, ())]
        pump.run(length, needed, call)

    for index in range(features // width):
        run(1.2, functools.partial(narrow_grads, index), (index % 2, 1))
    for tile in range(tiles):
        run(3.0, functools.partial(feed, tile), (tile % 2, 0))
    run(3.0, pull_middle)
    load_turned = load_tall()
    for index in range(features // width):
        run(1.0, functools.partial(contract_grads, index), (index % 2, 2))
    for group in range(groups):
        run(4.0, functools.partial(mix, group))
        run(2.5, functools.partial(unmix, group))
        run(1.5, functools.partial(expand_grads, group), (group % 2, 0))
    run(0.5, gating_grads)
    run(3.0, finish)
    pump.finish()
    for piece in pieces:
        for stage in range(1, bits):
            exchange(piece, stage).wait_send()
    pltpu.make_async_copy(middle_low, tokens_grad_out, out_sem.at[0]).wait()
    total = partial[0]
    for phase, members in enumerate(cube.circles()):
        weights = [1 << (len(members) - 1 - i) for i in range(len(members))]
        mine = sum(place[bit] * weight for bit, weight in zip(members, weights))
        partial[phase] = total
        other[phase, mine] = total
        copies = []
        for turn, flipped in enumerate(cube.subsets(members)):
            copy = pltpu.make_async_remote_copy(
                src_ref=partial.at[phase],
                dst_ref=other.at[phase, mine],
                send_sem=norm_send.at[phase, turn],
                recv_sem=norm_recv.at[phase, mine],
                device_id=cube.beyond(place, flipped),
                device_id_type=MESH,
            )
            copy.start()
            copies.append((copy, flipped))
        for copy, flipped in copies:
            theirs = sum(
                (1 - place[bit] if bit in flipped else place[bit]) * weight
                for bit, weight in zip(members, weights)
            )
            copy.wait_send()
            pltpu.make_async_remote_copy(
                src_ref=partial.at[phase],
                dst_ref=other.at[phase, theirs],
                send_sem=norm_send.at[phase, 0],
                recv_sem=norm_recv.at[phase, theirs],
                device_id=cube.beyond(place, flipped),
                device_id_type=MESH,
            ).wait_recv()
        total = other[phase, 0]
        for spot in range(1, 1 << len(members)):
            total = total + other[phase, spot]
    norm[...] = total


def backward_all(cube, streamed, kept, shapes, width=256):
    places, features = streamed[0].shape
    hidden, channels = streamed[2].shape[0], streamed[5].shape[0]
    kinds = [jnp.float32] + [BRAIN] * 5
    most = max(1 << len(members) for members in cube.circles())
    scratch = []
    for stage in range(cube.bits):
        scratch += [((2,) * (cube.bits - 1 - stage) + s, k) for s, k in zip(shapes, kinds)]
    pair = (2,) * cube.bits
    (rows_e, rows_g, rows_c, rows_n) = (shapes[i][0] for i in (1, 2, 3, 5))
    scratch += [
        ((2,) + pair + (rows_e, 2 * width), BRAIN),
        ((2,) + pair + (rows_n, width), BRAIN),
        ((2,) + pair + (rows_c, width), BRAIN),
        (pair + shapes[2], BRAIN),
        (pair + shapes[0], jnp.float32),
        ((channels, shapes[2][1]), BRAIN),
        ((places, features), BRAIN),
        ((features, places), BRAIN),
        ((hidden, places), BRAIN),
        ((places, features), jnp.float32),
        ((places, features), jnp.float32),
        ((places, features), BRAIN),
        ((10, places, width), jnp.float32),
        ((2, features, 2 * width), BRAIN),
        ((2, width, features), BRAIN),
        ((2, places, width), BRAIN),
        ((2, places, 2 * width), BRAIN),
        ((places, width), BRAIN),
        ((places, width), BRAIN),
        ((places, width), jnp.float32),
        ((places, width), jnp.float32),
        ((8, channels), jnp.float32),
        ((8, features), jnp.float32),
        ((2, 8, LANES), jnp.float32),
        ((2, most, 8, LANES), jnp.float32),
    ]
    count = 2 * (2 * features // width + hidden // width + channels // width) + 8
    sems = [(count, cube.bits)] * 2 + [(6,), (10,), (2, 2), (2,), (2,), (2, most), (2, most), (1,), (2,)]
    outs = [((places, features), BRAIN)] + [(s, jnp.float32) for s in shapes] + [((8, LANES), jnp.float32)]
    return pl.pallas_call(
        functools.partial(backward_kernel, cube, width),
        out_shape=[jax.ShapeDtypeStruct(*like) for like in outs],
        in_specs=[pl.BlockSpec(memory_space=pl.ANY)] * len(streamed)
        + [pl.BlockSpec(memory_space=pltpu.VMEM)] * len(kept),
        out_specs=[pl.BlockSpec(memory_space=pl.ANY)]
        + [pl.BlockSpec(memory_space=pltpu.VMEM)] * (len(outs) - 1),
        scratch_shapes=[pltpu.VMEM(*like) for like in scratch]
        + [pltpu.SemaphoreType.DMA(shape) for shape in sems],
        compiler_params=pltpu.CompilerParams(
            collective_id=3, has_side_effects=True, vmem_limit_bytes=BACK_BYTES
        ),
    )(*streamed, *kept)


PRODUCT_ROWS = 1024
BACK_BYTES = 63 * 1024 * 1024


def product_cols(former, latter):
    return lax.dot_general(
        former, latter, (((1,), (1,)), ((), ())), preferred_element_type=jnp.float32
    )


def adam_update(master, moment_one, moment_two, gradient, factor, rate, decay):
    clipped = gradient * factor
    new_one = BETA_FIRST * moment_one + (1.0 - BETA_FIRST) * clipped
    new_two = BETA_SECOND * moment_two + (1.0 - BETA_SECOND) * clipped * clipped
    first_hat = new_one / (1.0 - BETA_FIRST**STEP)
    second_hat = new_two / (1.0 - BETA_SECOND**STEP)
    after = master - rate * (first_hat / (jnp.sqrt(second_hat) + ADAM_EPSILON) + decay * master)
    return (after, new_one, new_two)


def product_rows(former, latter):
    return lax.dot_general(
        former, latter, (((0,), (0,)), ((), ())), preferred_element_type=jnp.float32
    )


def block_plain(cube, tokens, upstream, lengths, vectors, matrices, vector_rows):
    rows_t, rows_s = vector_rows
    expand, gating, contract, widen, narrow, vectors = (
        lax.all_gather(v, AXES, axis=0, tiled=True) for v in [m.astype(BRAIN) for m in matrices] + [vectors]
    )
    vectors = vectors.reshape(-1, 8, LANES).transpose(1, 0, 2)
    vec = channel_rows(vectors[:, :, :rows_t].reshape(8, -1))
    gains = vectors[:, :, rows_t : rows_t + rows_s].reshape(8, -1)
    masks = keep_masks(lengths[0], tokens.shape[0])
    normed, u, branch, recur, inlet, conv, state, mixed, middle, normed_two = mixer_forward(
        tokens, gains[0:1], gains[1:2], vec, masks, expand, gating, contract
    )
    gate, up = jnp.split(jnp.dot(normed_two, widen, preferred_element_type=jnp.float32), 2, axis=1)
    half, slope = gelu_parts(gate)
    active = (gate * half * up).astype(BRAIN)
    block_out = (middle + jnp.dot(active, narrow, preferred_element_type=jnp.float32)).astype(BRAIN)
    narrow_grad = product_rows(active, upstream)
    active_grad = product_cols(upstream, narrow)
    widened_grad = jnp.concatenate([active_grad * up * slope, active_grad * (gate * half)], axis=1).astype(BRAIN)
    widen_grad = product_rows(normed_two, widened_grad)
    middle_pull, scale_two_grad = rms_pull(middle, gains[1], product_cols(widened_grad, widen))
    middle_grad = upstream.astype(jnp.float32) + middle_pull
    middle_low = middle_grad.astype(BRAIN)
    contract_grad = product_rows(mixed, middle_low)
    projected_low, gating_grad, temporal_grad = mixer_backward(
        middle_low, contract, gating, vec, masks, u, branch, recur, inlet, conv, state
    )
    expand_grad = product_rows(normed, projected_low)
    tokens_pull, scale_one_grad = rms_pull(
        tokens.astype(jnp.float32), gains[0], product_cols(projected_low, expand)
    )
    tokens_grad = (middle_grad + tokens_pull).astype(BRAIN)
    devices = 1 << cube.bits
    scales_grad = jnp.pad(jnp.stack([scale_one_grad, scale_two_grad]), ((0, 6), (0, 0)))
    misc = [temporal_grad.reshape(8, devices, rows_t), scales_grad.reshape(8, devices, rows_s)]
    misc = jnp.pad(jnp.concatenate(misc, axis=2), ((0, 0), (0, 0), (0, LANES - rows_t - rows_s)))
    misc = misc.transpose(1, 0, 2).reshape(devices * 8, LANES)
    sums, norm = scatter_plain([misc, expand_grad, gating_grad, contract_grad, widen_grad, narrow_grad])
    return block_out, tokens_grad, sums, norm


def block_kernels(cube, tokens, upstream, lengths, vectors, matrices, vector_rows):
    fulls, outs = forward_all(cube, lengths, tokens, upstream, vectors, matrices, vector_rows)
    expand, gating, contract, widen, _ = fulls
    (u, branch, recur, inlet, state, conv, normed_t, mixed_t) = outs[:8]
    (pulled, active_t, block_out, middle, normed_two_t, vec, gains, masks) = outs[8:]
    streamed = (
        upstream, normed_two_t, active_t, pulled, widen, contract, expand,
        middle, normed_t, mixed_t, tokens, u, branch, recur, inlet, state, conv,
    )
    shapes = [v.shape for v in (vectors, *matrices)]
    outs = backward_all(cube, streamed, (gating, vec, gains, masks), shapes)
    return block_out, outs[0], outs[1:-1], outs[-1]


def shards(
    cube,
    tokens,
    cotangent,
    doc_lengths,
    expand,
    expand_mean,
    expand_square,
    contract,
    contract_mean,
    contract_square,
    gating,
    gating_mean,
    gating_square,
    widen,
    widen_mean,
    widen_square,
    narrow,
    narrow_mean,
    narrow_square,
    scales,
    scales_mean,
    scales_square,
    temporal,
    temporal_mean,
    temporal_square,
):
    rows_t, rows_s = temporal.shape[0], scales.shape[0]
    vectors = pack_vectors(temporal, scales).astype(BRAIN).astype(jnp.float32)
    matrices = (expand, gating, contract, widen, narrow)
    block = block_kernels if divides([m.shape[0] for m in matrices]) else block_plain
    block_out, tokens_grad, sums, norm_tile = block(
        cube, tokens[0], cotangent[0], doc_lengths, vectors, matrices, (rows_t, rows_s)
    )
    grads = list(sums[1:]) + [sums[0]]
    outs = adam_all(
        norm_tile,
        grads,
        (expand, gating, contract, widen, narrow, scales.T, temporal.T),
        (expand_mean, gating_mean, contract_mean, widen_mean, narrow_mean, scales_mean.T, temporal_mean.T),
        (
            expand_square,
            gating_square,
            contract_square,
            widen_square,
            narrow_square,
            scales_square.T,
            temporal_square.T,
        ),
    )
    grad_norm, outs = outs[0][0, 0], outs[1:]
    outs = [v.T if i % 7 > 4 else v for i, v in enumerate(outs)]
    updated = [outs[i + 7 * j] for i in (0, 2, 1, 3, 4, 5, 6) for j in range(3)]
    return (block_out[None], tokens_grad[None], grad_norm, *updated)


def solution(mesh):
    placed = (
        P(("dp", "fsdp"), None, None),
        P(("dp", "fsdp"), None, None),
        P(("dp", "fsdp"), None),
        P(("dp", "fsdp"), None),
        P(("dp", "fsdp"), None),
        P(("dp", "fsdp"), None),
        P(("dp", "fsdp"), None),
        P(("dp", "fsdp"), None),
        P(("dp", "fsdp"), None),
        P(("dp", "fsdp"), None),
        P(("dp", "fsdp"), None),
        P(("dp", "fsdp"), None),
        P(("dp", "fsdp"), None),
        P(("dp", "fsdp"), None),
        P(("dp", "fsdp"), None),
        P(("dp", "fsdp"), None),
        P(("dp", "fsdp"), None),
        P(("dp", "fsdp"), None),
        P(("dp", "fsdp"), None),
        P(("dp", "fsdp"), None),
        P(("dp", "fsdp"), None),
        P(("dp", "fsdp"), None),
        P(("dp", "fsdp"), None),
        P(("dp", "fsdp"), None),
    )
    return jax.shard_map(
        functools.partial(shards, Cube(mesh.shape)),
        mesh=mesh,
        in_specs=placed,
        out_specs=(
            P(("dp", "fsdp"), None, None),
            P(("dp", "fsdp"), None, None),
            P(),
            P(("dp", "fsdp"), None),
            P(("dp", "fsdp"), None),
            P(("dp", "fsdp"), None),
            P(("dp", "fsdp"), None),
            P(("dp", "fsdp"), None),
            P(("dp", "fsdp"), None),
            P(("dp", "fsdp"), None),
            P(("dp", "fsdp"), None),
            P(("dp", "fsdp"), None),
            P(("dp", "fsdp"), None),
            P(("dp", "fsdp"), None),
            P(("dp", "fsdp"), None),
            P(("dp", "fsdp"), None),
            P(("dp", "fsdp"), None),
            P(("dp", "fsdp"), None),
            P(("dp", "fsdp"), None),
            P(("dp", "fsdp"), None),
            P(("dp", "fsdp"), None),
            P(("dp", "fsdp"), None),
            P(("dp", "fsdp"), None),
            P(("dp", "fsdp"), None),
        ),
        check_vma=False,
    )
```
